32 devices in a mesh: doc: 4 (over y, x), term: 4 (over z), pair: 2 (over core).
Axes of the slice: x: 2, y: 2, z: 4, core: 2. Of those that a mesh axis runs over, the one named last changes fastest.
Arguments:
- counts: int32 [8, 16, 128, 128], P('doc', 'term'), may hold values from 0 to 11
- block_ids: int32 [8, 16], P('doc', 'term'), may hold values from 0 to 8191, as said below
- live_slots: int32 [8, 16], P('doc', 'term'), may hold values 0 or 1
- lengths: int32 [1024], P('doc'), may hold values from 1 to 24528, as said below
- pairs: int32 [512, 2], P(('doc', 'pair')), may hold values from 0 to 7, as said below
- pair_count: int32 [8], P(('doc', 'pair')), may hold values from 1 to 64, as said below
Outputs:
- gram: float32 [512, 128, 128], P(('doc', 'pair'), 'term')
The draws below stay inside these ranges and needn't reach their ends.
Inputs may be any that keep to these rules, and one draw needn't show every extreme that they name: `block_ids`: columns s * 4 to (s + 1) * 4 - 1 hold term blocks of the s-th of 4 equal ranges of the 8192 blocks, distinct within one document block and range. `lengths`: document b * 128 + r has a length of the sum of counts[b, s, r, t] over all slots s and all t plus tokens outside its blocks: 1 to 2000 of them for every document but the last, whose length is exactly 24528. `pairs`: the left block of row k belongs to doc index k // 128. Rows k with k % 64 < pair_count[k // 64] are live; some entry equals 64.
All inputs are finite; a program needn't handle non-finite values. No bound on the sum of `live_slots` on one device may be relied on, other than what follows from the above.
Results may differ from the reference program's by a relative error of at most 0.0014.
Values may be sent and summed in bfloat16 or wider, within the bound.
A program may use at most 64 MiB of HBM per device.

```python
import jax
import jax.numpy as jnp
from jax import lax

V = 1048576
TBLK = 128
DOCBLK = 128
DB_DEV = 2
TERM_BLOCK_SLOTS = 4
PAIR_DEV = 64
TERM_BLOCKS = 8192
NDB = 8
DOCS = 1024
TSLOTS = 16
NPAIRS = 512
N_DOC = 4
N_TERM = 4
N_PAIR = 2


def draw_block_ids(key, part):
    covered_blocks = V // TBLK // N_TERM
    perm_keys = jax.random.split(jax.random.fold_in(key, 21), N_TERM)
    ordering = jax.vmap(lambda part_key: jax.random.permutation(part_key, covered_blocks))(perm_keys)
    ranking_order = jnp.argsort(ordering, axis=1).astype(jnp.int32)
    extra_score = jnp.where(ranking_order < 2 * TERM_BLOCK_SLOTS, 2 ** 18, 0).astype(jnp.int32)
    jitter_score = jax.random.randint(jax.random.fold_in(key, 22), (NDB, N_TERM, covered_blocks), 0, 2 ** 18)
    complete_score = (jitter_score + extra_score[None]) * covered_blocks + jnp.arange(covered_blocks, dtype=jnp.int32)
    picked = lax.top_k(complete_score, TERM_BLOCK_SLOTS)[1].astype(jnp.int32)
    global_ids = picked + (jnp.arange(N_TERM, dtype=jnp.int32) * covered_blocks)[None, :, None]
    return global_ids.reshape(NDB, N_TERM * TERM_BLOCK_SLOTS).astype(jnp.int32)


def count_grid(key):
    slot_total = TERM_BLOCK_SLOTS * N_TERM
    grid_shape = (NDB, slot_total, DOCBLK, TBLK)
    slot_blocks = draw_block_ids(key, 0)
    term_level = jax.random.randint(jax.random.fold_in(key, 14), (TERM_BLOCKS, TBLK), 300, 1001)
    slot_level = jax.random.randint(jax.random.fold_in(key, 15), (NDB, slot_total), 500, 1001)
    level = term_level[slot_blocks] * slot_level[:, :, None] // 1000
    doc_index = jnp.arange(NDB, dtype=jnp.int32)[:, None, None, None] * DOCBLK + jnp.arange(DOCBLK, dtype=jnp.int32)[None, None, :, None]
    thresh = level[:, :, None, :] * (DOCS + 2 * doc_index) // (2 * DOCS)
    coin_flip = jax.random.randint(jax.random.fold_in(key, 11), grid_shape, 0, 1000)
    ceiling = jax.random.randint(jax.random.fold_in(key, 12), grid_shape, 2, 13)
    count_value = jax.random.randint(jax.random.fold_in(key, 13), grid_shape, 1, ceiling)
    return jnp.where(coin_flip < thresh, count_value, 0).astype(jnp.int32)


def draw_counts(key, part):
    return count_grid(key)


def draw_lengths(key, part):
    grid = count_grid(key)
    inside = jnp.sum(grid, axis=(1, 3)).reshape(DOCS)
    block_top = jax.random.randint(jax.random.fold_in(key, 32), (NDB,), 2, 2002)
    doc_top = jnp.repeat(block_top, DOCBLK)
    outside = jax.random.randint(jax.random.fold_in(key, 31), (DOCS,), 1, doc_top)
    top_length = 11 * TERM_BLOCK_SLOTS * N_TERM * TBLK + 2000
    outside = outside.at[DOCS - 1].set(top_length - inside[DOCS - 1])
    return (inside + outside).astype(jnp.int32)


def draw_pairs(key, part):
    row_index = jnp.arange(NPAIRS, dtype=jnp.int32)
    owner_index = row_index // (PAIR_DEV * N_PAIR)
    left_block = owner_index * DB_DEV + jax.random.randint(jax.random.fold_in(key, 41), (NPAIRS,), 0, DB_DEV)
    right_block = jax.random.randint(jax.random.fold_in(key, 42), (NPAIRS,), 0, NDB)
    return jnp.stack([left_block, right_block], axis=1).astype(jnp.int32)


def draw_pair_count(key, part):
    heavy_side = jax.random.randint(jax.random.fold_in(key, 51), (N_DOC,), 0, N_PAIR)
    heavy_count = jax.random.randint(jax.random.fold_in(key, 52), (N_DOC,), 3 * PAIR_DEV // 4, PAIR_DEV + 1)
    heavy_count = heavy_count.at[0].set(PAIR_DEV)
    light_count = jax.random.randint(jax.random.fold_in(key, 53), (N_DOC, N_PAIR), 1, PAIR_DEV // 4 + 1)
    side_index = jnp.arange(N_PAIR, dtype=jnp.int32)[None, :]
    return jnp.where(side_index == heavy_side[:, None], heavy_count[:, None], light_count).reshape(-1).astype(jnp.int32)


def place_ends(drawn, own_key, low, largest):
    spot = [jax.random.randint(jax.random.fold_in(own_key, axis), (), 0, length) for axis, length in enumerate(drawn.shape)]
    longest = drawn.shape.index(max(drawn.shape))
    beside = spot[:longest] + [(spot[longest] + 1) % drawn.shape[longest]] + spot[longest + 1:]
    return drawn.at[tuple(spot)].set(low).at[tuple(beside)].set(largest)


def setup_inputs(seed: int = 0) -> dict:
    splits = jax.random.split(jax.random.key(seed), 7)
    counts = draw_counts(jax.random.fold_in(splits[6], 71), 0)
    block_ids = draw_block_ids(jax.random.fold_in(splits[6], 71), 0)
    live_slots = place_ends((jax.random.randint(splits[2], (NDB, TSLOTS), 0, 4) < 3).astype(jnp.int32), jax.random.fold_in(splits[2], 1), 0, 1)
    lengths = draw_lengths(jax.random.fold_in(splits[6], 71), 0)
    pairs = draw_pairs(jax.random.fold_in(splits[6], 71), 0)
    pair_count = draw_pair_count(jax.random.fold_in(splits[6], 71), 0)
    return dict(counts=counts, block_ids=block_ids, live_slots=live_slots, lengths=lengths, pairs=pairs, pair_count=pair_count)


saturation = 1.2
length_weight = 0.75
epsilon = 1e-06

def reference(counts, block_ids, live_slots, lengths, pairs, pair_count):
    present = (counts > 0) & (live_slots[:, :, None, None] > 0)
    col_docs = lax.optimization_barrier(jnp.sum(present.astype(jnp.float32), axis=2))
    doc_freq = jnp.zeros((TERM_BLOCKS, TBLK), jnp.float32).at[block_ids.reshape(-1)].add(col_docs.reshape(-1, TBLK))
    len_float = lengths.astype(jnp.float32)
    avg_len = jnp.sum(len_float) / DOCS
    inv_freq = jnp.log(1.0 + (DOCS - doc_freq + 0.5) / (doc_freq + 0.5))
    slot_freq = inv_freq[block_ids]
    len_scale = 1.0 - length_weight + length_weight * len_float.reshape(NDB, 1, DOCBLK, 1) / avg_len
    term_freq = counts.astype(jnp.float32)
    weight = jnp.where(present, slot_freq[:, :, None, :] * term_freq * (saturation + 1.0) / (term_freq + saturation * len_scale), 0.0)
    square_sum = lax.optimization_barrier(jnp.sum(weight * weight, axis=(1, 3)))
    normalized = (weight * lax.rsqrt(square_sum + epsilon)[:, None, :, None]).astype(jnp.bfloat16)
    row_index = jnp.arange(NPAIRS, dtype=jnp.int32)
    live_pair = row_index % PAIR_DEV < pair_count[row_index // PAIR_DEV]

    def one_pair(item):
        pair_row, live_flag = item
        left_tiles = normalized[pair_row[0]].astype(jnp.float32)
        right_tiles = normalized[pair_row[1]].astype(jnp.float32)
        matches = (block_ids[pair_row[0]][:, None] == block_ids[pair_row[1]][None, :]).astype(jnp.float32)
        aligned = jnp.einsum('ij,jet->iet', matches, right_tiles)
        gram_tile = jnp.einsum('idt,iet->de', left_tiles, aligned)
        return jnp.where(live_flag, gram_tile, 0.0)
    return lax.map(one_pair, (pairs, live_pair))
```

```python
import functools

import jax
import jax.numpy as jnp
from jax import lax
from jax.experimental import pallas as pl
from jax.experimental.pallas import tpu as pltpu
from jax.sharding import PartitionSpec as P

saturation = 1.2
length_weight = 0.75
epsilon = 1e-06

MESH = pl.DeviceIdType.MESH


def tiles_kernel(
    sizes,
    live_ref,
    ids_ref,
    counts_ref,
    lengths_ref,
    out_ref,
    masked,
    small,
    right_counts,
    left_weight,
    right_weight,
    partial_sum,
    term_recv,
    square_own,
    square_recv,
    column,
    final,
    pair_recv,
    small_send_sem,
    small_recv_sem,
    count_send_sem,
    count_recv_sem,
    term_send_sem,
    term_recv_sem,
    square_send_sem,
    square_recv_sem,
    pair_send_sem,
    pair_recv_sem,
):
    n_doc, n_term, n_pair = sizes
    blocks, slots, rows, cols = counts_ref.shape
    per_core = blocks // n_pair
    n_right = n_doc * per_core
    part_rows = rows // n_term
    docs_all = n_doc * blocks * rows
    me_doc = lax.axis_index("doc")
    me_term = lax.axis_index("term")
    me_pair = lax.axis_index("pair")

    def doc_peer(k):
        return {"doc": lax.rem(me_doc + k, n_doc)}

    def term_peer(k):
        return {"term": lax.rem(me_term + k, n_term)}

    def pair_peer(k):
        return {"pair": lax.rem(me_pair + k, n_pair)}

    def small_copy(k):
        return pltpu.make_async_remote_copy(
            src_ref=small.at[0],
            dst_ref=small.at[k],
            send_sem=small_send_sem.at[k],
            recv_sem=small_recv_sem.at[k],
            device_id=doc_peer(k),
            device_id_type=MESH,
        )

    def count_copy(k):
        return pltpu.make_async_remote_copy(
            src_ref=masked.at[pl.ds(me_pair * per_core, per_core)],
            dst_ref=right_counts.at[k],
            send_sem=count_send_sem.at[k],
            recv_sem=count_recv_sem.at[k],
            device_id=doc_peer(k),
            device_id_type=MESH,
        )

    def term_copy(m, k):
        return pltpu.make_async_remote_copy(
            src_ref=partial_sum.at[m, lax.rem(me_term + k, n_term)],
            dst_ref=term_recv.at[m, k],
            send_sem=term_send_sem.at[m, k],
            recv_sem=term_recv_sem.at[m, k],
            device_id=term_peer(k),
            device_id_type=MESH,
        )

    def square_copy(k):
        return pltpu.make_async_remote_copy(
            src_ref=square_own,
            dst_ref=square_recv.at[k],
            send_sem=square_send_sem.at[k],
            recv_sem=square_recv_sem.at[k],
            device_id=term_peer(k),
            device_id_type=MESH,
        )

    def pair_copy(m, k):
        return pltpu.make_async_remote_copy(
            src_ref=final.at[m],
            dst_ref=pair_recv.at[k, m],
            send_sem=pair_send_sem.at[m, k],
            recv_sem=pair_recv_sem.at[m, k],
            device_id=pair_peer(k),
            device_id_type=MESH,
        )

    barrier = pltpu.get_barrier_semaphore()
    for k in range(1, n_doc):
        pl.semaphore_signal(barrier, inc=1, device_id=doc_peer(k), device_id_type=MESH)
    for k in range(1, n_term):
        pl.semaphore_signal(barrier, inc=1, device_id=term_peer(k), device_id_type=MESH)
    for k in range(1, n_pair):
        pl.semaphore_signal(barrier, inc=1, device_id=pair_peer(k), device_id_type=MESH)

    small[0] = jnp.zeros(small.shape[1:], jnp.float32)
    for b in range(blocks):
        for s in range(slots):
            live = jnp.full((rows, cols), live_ref[b, s], jnp.int32) > 0
            value = jnp.where(live, counts_ref[b, s].astype(jnp.float32), 0.0)
            masked[b, s] = value.astype(jnp.bfloat16)
            small[0, b, s : s + 1] = jnp.sum(
                jnp.where(value > 0.0, 1.0, 0.0), axis=0, keepdims=True
            )
            small[0, b, slots + s : slots + s + 1] = jnp.full(
                (1, cols), ids_ref[b, s], jnp.int32
            ).astype(jnp.float32)
    small[0, blocks, 0:blocks] = lengths_ref[...].astype(jnp.float32)
    square_own[...] = jnp.zeros(square_own.shape, jnp.float32)

    pl.semaphore_wait(barrier, n_doc + n_term + n_pair - 3)

    for k in range(1, n_doc):
        small_copy(k).start()
    for k in range(1, n_doc):
        count_copy(k).start()
    for k in range(1, n_doc):
        small_copy(k).wait_recv()

    total_len = lax.fori_loop(
        0,
        n_doc,
        lambda k, acc: acc + jnp.sum(small[k, blocks], axis=0, keepdims=True),
        jnp.zeros((1, cols), jnp.float32),
    )
    avg_len = jnp.sum(total_len, axis=1, keepdims=True) / docs_all

    def inv_freq_of(ids):
        def add(k, acc):
            for b in range(blocks):
                table = small[k, b]
                for s in range(slots):
                    same = ids == table[slots + s : slots + s + 1]
                    acc = acc + jnp.where(same, table[s : s + 1], 0.0)
            return acc

        freq = lax.fori_loop(0, n_doc, add, jnp.zeros(ids.shape, jnp.float32))
        return jnp.log(1.0 + (docs_all - freq + 0.5) / (freq + 0.5))

    def weigh(k, b, read, target, square_row):
        inv_freq = inv_freq_of(small[k, b, slots : 2 * slots]) * (saturation + 1.0)
        length = small[k, blocks, pl.ds(b, 1)]
        scale = saturation * (1.0 - length_weight + length_weight * length / avg_len)
        scale = jnp.transpose(jnp.broadcast_to(scale, (rows, rows)))
        squares = jnp.zeros((rows, cols), jnp.float32)
        for s in range(slots):
            freq = read(s).astype(jnp.float32)
            weight = inv_freq[s : s + 1] * freq / (freq + scale)
            squares = squares + weight * weight
            target[s] = weight.astype(jnp.bfloat16)
        square_own[pl.ds(square_row, 1)] = jnp.sum(
            jnp.transpose(squares), axis=0, keepdims=True
        )

    for b in range(blocks):
        weigh(0, b, lambda s, b=b: masked[b, s], left_weight.at[b], b)

    def grams(m, right, right_ids):
        for b in range(blocks):
            left_ids = small[0, b, slots : 2 * slots]
            gram = jnp.zeros((rows, rows), jnp.float32)
            for i in range(slots):
                aligned = jnp.zeros((rows, cols), jnp.bfloat16)
                for j in range(slots):
                    same = left_ids[i : i + 1] == right_ids[j : j + 1]
                    same = jnp.where(same, 1.0, 0.0).astype(jnp.bfloat16)
                    aligned = aligned + right[j] * same
                gram = gram + lax.dot_general(
                    left_weight[b, i],
                    aligned,
                    (((1,), (1,)), ((), ())),
                    preferred_element_type=jnp.float32,
                )
            for z in range(n_term):
                partial_sum[m, z, b] = gram[z * part_rows : (z + 1) * part_rows]
        for k in range(1, n_term):
            term_copy(m, k).start()

    for i in range(per_core):
        own = me_pair * per_core + i
        square_own[pl.ds(blocks + i, 1)] = square_own[pl.ds(own, 1)]
        grams(i, left_weight.at[own], small[0, own, slots : 2 * slots])

    def right_step(k, carry):
        count_copy(k).wait_recv()
        for i in range(per_core):
            b = me_pair * per_core + i
            m = k * per_core + i
            weigh(k, b, lambda s, i=i: right_counts[k, i, s], right_weight, blocks + m)

            @pl.when(m == n_right - 1)
            def _():
                for t in range(1, n_term):
                    square_copy(t).start()

            grams(m, right_weight, small[k, b, slots : 2 * slots])
        return carry

    lax.fori_loop(1, n_doc, right_step, 0)

    squares = square_own[...]
    for k in range(1, n_term):
        square_copy(k).wait_recv()
        squares = squares + square_recv[k]
    inverse = lax.rsqrt(squares + epsilon)
    square_own_done = [square_copy(k) for k in range(1, n_term)]
    for copy in square_own_done:
        copy.wait_send()
    square_own[...] = inverse
    left_scale = []
    for b in range(blocks):
        column[...] = jnp.transpose(jnp.broadcast_to(inverse[b : b + 1], (rows, rows)))
        left_scale.append(column[pl.ds(me_term * part_rows, part_rows)])

    def finish(m, carry):
        for k in range(1, n_term):
            term_copy(m, k).wait_recv()
        right_scale = square_own[pl.ds(blocks + m, 1)]
        for b in range(blocks):
            total = partial_sum[m, me_term, b]
            for k in range(1, n_term):
                total = total + term_recv[m, k, b]
            value = total * left_scale[b] * right_scale
            final[m, b] = value
            out_ref[0, m, b] = value
        for k in range(1, n_pair):
            pair_copy(m, k).start()
        return carry

    lax.fori_loop(0, n_right, finish, 0)

    def collect(m, carry):
        for k in range(1, n_pair):
            pair_copy(m, k).wait_recv()
            out_ref[k, m] = pair_recv[k, m]
        for k in range(1, n_term):
            term_copy(m, k).wait_send()
        for k in range(1, n_pair):
            pair_copy(m, k).wait_send()
        return carry

    lax.fori_loop(0, n_right, collect, 0)
    for k in range(1, n_doc):
        small_copy(k).wait_send()
        count_copy(k).wait_send()


def place_kernel(sizes, blocks, pairs_ref, count_ref, tiles_ref, out_ref):
    n_doc, n_term, n_pair = sizes
    per_core = blocks // n_pair
    me_doc = lax.axis_index("doc")
    me_pair = lax.axis_index("pair")
    count = count_ref[0]

    def step(row, carry):
        live = row < count

        @pl.when(live)
        def _():
            left = pairs_ref[0, row] - me_doc * blocks
            right = pairs_ref[1, row]
            owner, inner = right // blocks, right % blocks
            side = lax.rem(me_pair - inner // per_core + n_pair, n_pair)
            m = lax.rem(me_doc - owner + n_doc, n_doc) * per_core + inner % per_core
            out_ref[row] = tiles_ref[side, m, left]

        @pl.when(jnp.logical_not(live))
        def _():
            out_ref[row] = jnp.zeros(out_ref.shape[1:], jnp.float32)

        return carry

    lax.fori_loop(0, out_ref.shape[0], step, 0, unroll=4)


def shards(sizes, counts, block_ids, live_slots, lengths, pairs, pair_count):
    n_doc, n_term, n_pair = sizes
    blocks, slots, rows, cols = counts.shape
    per_core = blocks // n_pair
    n_right = n_doc * per_core
    part_rows = rows // n_term
    table_rows = -(-max(2 * slots, blocks) // 8) * 8
    square_rows = -(-(blocks + n_right) // 8) * 8
    dma = pltpu.SemaphoreType.DMA
    smem = pl.BlockSpec(memory_space=pltpu.SMEM)
    vmem = pl.BlockSpec(memory_space=pltpu.VMEM)
    tiles = pl.pallas_call(
        functools.partial(tiles_kernel, sizes),
        out_shape=jax.ShapeDtypeStruct((n_pair, n_right, blocks, part_rows, rows), jnp.float32),
        in_specs=[smem, smem, vmem, vmem],
        out_specs=vmem,
        scratch_shapes=[
            pltpu.VMEM((blocks, slots, rows, cols), jnp.bfloat16),
            pltpu.VMEM((n_doc, blocks + 1, table_rows, cols), jnp.float32),
            pltpu.VMEM((n_doc, per_core, slots, rows, cols), jnp.bfloat16),
            pltpu.VMEM((blocks, slots, rows, cols), jnp.bfloat16),
            pltpu.VMEM((slots, rows, cols), jnp.bfloat16),
            pltpu.VMEM((n_right, n_term, blocks, part_rows, rows), jnp.float32),
            pltpu.VMEM((n_right, n_term, blocks, part_rows, rows), jnp.float32),
            pltpu.VMEM((square_rows, rows), jnp.float32),
            pltpu.VMEM((n_term, square_rows, rows), jnp.float32),
            pltpu.VMEM((rows, rows), jnp.float32),
            pltpu.VMEM((n_right, blocks, part_rows, rows), jnp.float32),
            pltpu.VMEM((n_pair, n_right, blocks, part_rows, rows), jnp.float32),
            dma((n_doc,)),
            dma((n_doc,)),
            dma((n_doc,)),
            dma((n_doc,)),
            dma((n_right, n_term)),
            dma((n_right, n_term)),
            dma((n_term,)),
            dma((n_term,)),
            dma((n_right, n_pair)),
            dma((n_right, n_pair)),
        ],
        compiler_params=pltpu.CompilerParams(
            collective_id=0, has_side_effects=True, vmem_limit_bytes=48 * 1024 * 1024
        ),
    )(live_slots, block_ids, counts, lengths.reshape(blocks, rows))
    return pl.pallas_call(
        functools.partial(place_kernel, sizes, blocks),
        out_shape=jax.ShapeDtypeStruct((pairs.shape[0], part_rows, rows), jnp.float32),
        in_specs=[smem, smem, vmem],
        out_specs=vmem,
        compiler_params=pltpu.CompilerParams(vmem_limit_bytes=48 * 1024 * 1024),
    )(pairs.T, pair_count, tiles)


def solution(mesh):
    sizes = (mesh.shape["doc"], mesh.shape["term"], mesh.shape["pair"])
    in_specs = (
        P("doc", "term", None, None),
        P("doc", "term"),
        P("doc", "term"),
        P("doc"),
        P(("doc", "pair"), None),
        P(("doc", "pair")),
    )
    out_specs = P(("doc", "pair"), "term", None)
    return jax.shard_map(
        functools.partial(shards, sizes),
        mesh=mesh,
        in_specs=in_specs,
        out_specs=out_specs,
        check_vma=False,
    )
```

```python
import functools

import jax
import jax.numpy as jnp
from jax import lax
from jax.experimental import pallas as pl
from jax.experimental.pallas import tpu as pltpu
from jax.sharding import PartitionSpec as P

steps = 32767.0
tiny = 1e-30
saturation = 1.2
length_weight = 0.75
epsilon = 1e-06

MESH = pl.DeviceIdType.MESH


def tiles_kernel(
    sizes,
    live_hbm,
    ids_hbm,
    counts_hbm,
    lengths_hbm,
    out_ref,
    live_ref,
    ids_ref,
    counts_ref,
    lengths_ref,
    masked,
    small,
    right_counts,
    left_weight,
    right_weight,
    partial_sum,
    coded,
    scale_own,
    term_recv,
    scale_recv,
    square_own,
    square_recv,
    column,
    final,
    pair_recv,
    load_sem,
    small_send_sem,
    small_recv_sem,
    count_send_sem,
    count_recv_sem,
    term_send_sem,
    term_recv_sem,
    scale_send_sem,
    scale_recv_sem,
    square_send_sem,
    square_recv_sem,
    pair_send_sem,
    pair_recv_sem,
):
    n_doc, n_term, n_pair = sizes
    blocks, slots, rows, cols = counts_ref.shape
    per_core = blocks // n_pair
    n_right = n_doc * per_core
    part_rows = rows // n_term
    docs_all = n_doc * blocks * rows
    me_doc = lax.axis_index("doc")
    me_term = lax.axis_index("term")
    me_pair = lax.axis_index("pair")

    def doc_peer(k):
        return {"doc": lax.rem(me_doc + k, n_doc)}

    def term_peer(k):
        return {"term": lax.rem(me_term + k, n_term)}

    def pair_peer(k):
        return {"pair": lax.rem(me_pair + k, n_pair)}

    def small_copy(k):
        return pltpu.make_async_remote_copy(
            src_ref=small.at[0],
            dst_ref=small.at[k],
            send_sem=small_send_sem.at[k],
            recv_sem=small_recv_sem.at[k],
            device_id=doc_peer(k),
            device_id_type=MESH,
        )

    def count_copy(k):
        return pltpu.make_async_remote_copy(
            src_ref=masked.at[pl.ds(me_pair * per_core, per_core)],
            dst_ref=right_counts.at[k],
            send_sem=count_send_sem.at[k],
            recv_sem=count_recv_sem.at[k],
            device_id=doc_peer(k),
            device_id_type=MESH,
        )

    def term_copy(m, k):
        return pltpu.make_async_remote_copy(
            src_ref=coded.at[m, lax.rem(me_term + k, n_term)],
            dst_ref=term_recv.at[m, k],
            send_sem=term_send_sem.at[m, k],
            recv_sem=term_recv_sem.at[m, k],
            device_id=term_peer(k),
            device_id_type=MESH,
        )

    def scale_copy(k):
        return pltpu.make_async_remote_copy(
            src_ref=scale_own.at[lax.rem(me_term + k, n_term)],
            dst_ref=scale_recv.at[k],
            send_sem=scale_send_sem.at[k],
            recv_sem=scale_recv_sem.at[k],
            device_id=term_peer(k),
            device_id_type=MESH,
        )

    def square_copy(k):
        return pltpu.make_async_remote_copy(
            src_ref=square_own,
            dst_ref=square_recv.at[k],
            send_sem=square_send_sem.at[k],
            recv_sem=square_recv_sem.at[k],
            device_id=term_peer(k),
            device_id_type=MESH,
        )

    def pair_copy(m, k):
        return pltpu.make_async_remote_copy(
            src_ref=final.at[m],
            dst_ref=pair_recv.at[k, m],
            send_sem=pair_send_sem.at[m, k],
            recv_sem=pair_recv_sem.at[m, k],
            device_id=pair_peer(k),
            device_id_type=MESH,
        )

    barrier = pltpu.get_barrier_semaphore()
    for k in range(1, n_doc):
        pl.semaphore_signal(barrier, inc=1, device_id=doc_peer(k), device_id_type=MESH)
    for k in range(1, n_term):
        pl.semaphore_signal(barrier, inc=1, device_id=term_peer(k), device_id_type=MESH)
    for k in range(1, n_pair):
        pl.semaphore_signal(barrier, inc=1, device_id=pair_peer(k), device_id_type=MESH)

    loads = [
        pltpu.make_async_copy(live_hbm, live_ref, load_sem.at[0]),
        pltpu.make_async_copy(ids_hbm, ids_ref, load_sem.at[1]),
        pltpu.make_async_copy(lengths_hbm, lengths_ref, load_sem.at[2]),
    ]
    loads += [
        pltpu.make_async_copy(counts_hbm.at[b], counts_ref.at[b], load_sem.at[3 + b])
        for b in range(blocks)
    ]
    for load in loads:
        load.start()
    small[0] = jnp.zeros(small.shape[1:], jnp.float32)
    square_own[...] = jnp.zeros(square_own.shape, jnp.float32)
    out_ref[out_ref.shape[0] - 1] = jnp.zeros(out_ref.shape[1:], jnp.float32)
    for load in loads[:3]:
        load.wait()
    for b in range(blocks):
        loads[3 + b].wait()
        for s in range(slots):
            live = jnp.broadcast_to(live_ref[b : b + 1, s : s + 1], (rows, cols)) > 0
            value = jnp.where(live, counts_ref[b, s].astype(jnp.float32), 0.0)
            masked[b, s] = value.astype(jnp.bfloat16)
            small[0, b, s : s + 1] = jnp.sum(
                jnp.where(value > 0.0, 1.0, 0.0), axis=0, keepdims=True
            )
            small[0, b, slots + s : slots + s + 1] = jnp.broadcast_to(
                ids_ref[b : b + 1, s : s + 1], (1, cols)
            ).astype(jnp.float32)
    small[0, blocks, 0:blocks] = lengths_ref[...].astype(jnp.float32)

    pl.semaphore_wait(barrier, n_doc + n_term + n_pair - 3)

    for k in range(1, n_doc):
        small_copy(k).start()
    for k in range(1, n_doc):
        count_copy(k).start()
    for k in range(1, n_doc):
        small_copy(k).wait_recv()

    total_len = lax.fori_loop(
        0,
        n_doc,
        lambda k, acc: acc + jnp.sum(small[k, blocks], axis=0, keepdims=True),
        jnp.zeros((1, cols), jnp.float32),
    )
    avg_len = jnp.sum(total_len, axis=1, keepdims=True) / docs_all

    def inv_freq_of(ids):
        def add(k, acc):
            for b in range(blocks):
                table = small[k, b]
                for s in range(slots):
                    same = ids == table[slots + s : slots + s + 1]
                    acc = acc + jnp.where(same, table[s : s + 1], 0.0)
            return acc

        freq = lax.fori_loop(0, n_doc, add, jnp.zeros(ids.shape, jnp.float32))
        return jnp.log(1.0 + (docs_all - freq + 0.5) / (freq + 0.5))

    def weigh(k, b, read, target, square_row):
        inv_freq = inv_freq_of(small[k, b, slots : 2 * slots]) * (saturation + 1.0)
        length = small[k, blocks, pl.ds(b, 1)]
        scale = saturation * (1.0 - length_weight + length_weight * length / avg_len)
        scale = jnp.transpose(jnp.broadcast_to(scale, (rows, rows)))
        squares = jnp.zeros((rows, cols), jnp.float32)
        for s in range(slots):
            freq = read(s).astype(jnp.float32)
            weight = inv_freq[s : s + 1] * freq / (freq + scale)
            squares = squares + weight * weight
            target[s] = weight.astype(jnp.bfloat16)
        square_own[pl.ds(square_row, 1)] = jnp.sum(
            jnp.transpose(squares), axis=0, keepdims=True
        )

    for b in range(blocks):
        weigh(0, b, lambda s, b=b: masked[b, s], left_weight.at[b], b)

    def grams(m, right, right_ids):
        for b in range(blocks):
            left_ids = small[0, b, slots : 2 * slots]
            gram = jnp.zeros((rows, rows), jnp.float32)
            for i in range(slots):
                aligned = jnp.zeros((rows, cols), jnp.bfloat16)
                for j in range(slots):
                    same = left_ids[i : i + 1] == right_ids[j : j + 1]
                    same = jnp.where(same, 1.0, 0.0).astype(jnp.bfloat16)
                    aligned = aligned + right[j] * same
                gram = gram + lax.dot_general(
                    left_weight[b, i],
                    aligned,
                    (((1,), (1,)), ((), ())),
                    preferred_element_type=jnp.float32,
                )
            for z in range(n_term):
                piece = gram[z * part_rows : (z + 1) * part_rows]
                top = jnp.maximum(jnp.max(piece, axis=0, keepdims=True), tiny)
                partial_sum[m, z, b] = piece
                code = (piece * (steps / top) + 0.5).astype(jnp.int32)
                coded[m, z, b] = code.astype(jnp.int16)
                scale_own[z, pl.ds(m * blocks + b, 1)] = top * (1.0 / steps)
        for k in range(1, n_term):
            term_copy(m, k).start()

    for i in range(per_core):
        own = me_pair * per_core + i
        square_own[pl.ds(blocks + i, 1)] = square_own[pl.ds(own, 1)]
        grams(i, left_weight.at[own], small[0, own, slots : 2 * slots])

    def right_step(k, carry):
        count_copy(k).wait_recv()
        for i in range(per_core):
            b = me_pair * per_core + i
            m = k * per_core + i
            weigh(k, b, lambda s, i=i: right_counts[k, i, s], right_weight, blocks + m)

            @pl.when(m == n_right - 1)
            def _():
                for t in range(1, n_term):
                    square_copy(t).start()

            grams(m, right_weight, small[k, b, slots : 2 * slots])
        return carry

    lax.fori_loop(1, n_doc, right_step, 0)

    for k in range(1, n_term):
        scale_copy(k).start()
    squares = square_own[...]
    for k in range(1, n_term):
        square_copy(k).wait_recv()
        squares = squares + square_recv[k]
    inverse = lax.rsqrt(squares + epsilon)
    for k in range(1, n_term):
        square_copy(k).wait_send()
    square_own[...] = inverse
    left_scale = []
    for b in range(blocks):
        column[...] = jnp.transpose(jnp.broadcast_to(inverse[b : b + 1], (rows, rows)))
        left_scale.append(column[pl.ds(me_term * part_rows, part_rows)])

    for k in range(1, n_term):
        scale_copy(k).wait_recv()

    def finish(m, carry):
        for k in range(1, n_term):
            term_copy(m, k).wait_recv()
        right_scale = square_own[pl.ds(blocks + m, 1)]
        for b in range(blocks):
            total = partial_sum[m, me_term, b]
            for k in range(1, n_term):
                scale = scale_recv[k, pl.ds(m * blocks + b, 1)]
                total = total + term_recv[m, k, b].astype(jnp.float32) * scale
            value = total * left_scale[b] * right_scale
            final[m, b] = value
            out_ref[m * blocks + b] = value
        for k in range(1, n_pair):
            pair_copy(m, k).start()
        return carry

    lax.fori_loop(0, n_right, finish, 0)

    def collect(m, carry):
        for k in range(1, n_pair):
            pair_copy(m, k).wait_recv()
            out_ref[pl.ds((k * n_right + m) * blocks, blocks)] = pair_recv[k, m]
        for k in range(1, n_term):
            term_copy(m, k).wait_send()
        for k in range(1, n_pair):
            pair_copy(m, k).wait_send()
        return carry

    lax.fori_loop(0, n_right, collect, 0)
    for k in range(1, n_term):
        scale_copy(k).wait_send()
    for k in range(1, n_doc):
        small_copy(k).wait_send()
        count_copy(k).wait_send()


def place_kernel(sizes, blocks, pairs_ref, count_ref, tiles_ref, out_ref, first_tile, sem):
    n_doc, n_term, n_pair = sizes
    per_core = blocks // n_pair
    n_right = n_doc * per_core
    me_doc = lax.axis_index("doc")
    me_pair = lax.axis_index("pair")
    count = count_ref[0]
    zero_tile = tiles_ref.shape[0] - 1

    def fill(owner, carry):
        k = lax.rem(me_doc - owner + n_doc, n_doc)
        for inner in range(blocks):
            side = lax.rem(me_pair - inner // per_core + n_pair, n_pair)
            m = side * n_right + k * per_core + inner % per_core
            first_tile[owner * blocks + inner] = (m - me_doc) * blocks
        return carry

    lax.fori_loop(0, n_doc, fill, 0)

    def step(row, carry):
        tile = first_tile[pairs_ref[1, row]] + pairs_ref[0, row]
        tile = jnp.where(row < count, tile, zero_tile)
        pltpu.make_async_copy(tiles_ref.at[tile], out_ref.at[row], sem).start()
        return carry

    lax.fori_loop(0, out_ref.shape[0], step, 0, unroll=8)
    pltpu.make_async_copy(out_ref, out_ref, sem).wait()


def shards(sizes, counts, block_ids, live_slots, lengths, pairs, pair_count):
    n_doc, n_term, n_pair = sizes
    blocks, slots, rows, cols = counts.shape
    per_core = blocks // n_pair
    n_right = n_doc * per_core
    part_rows = rows // n_term
    table_rows = -(-max(2 * slots, blocks) // 8) * 8
    square_rows = -(-(blocks + n_right) // 8) * 8
    dma = pltpu.SemaphoreType.DMA
    scale_rows = -(-(blocks * n_right) // 8) * 8
    hbm = pl.BlockSpec(memory_space=pltpu.HBM)
    smem = pl.BlockSpec(memory_space=pltpu.SMEM)
    vmem = pl.BlockSpec(memory_space=pltpu.VMEM)
    tiles = pl.pallas_call(
        functools.partial(tiles_kernel, sizes),
        out_shape=pltpu.VMEM((n_pair * n_right * blocks + 1, part_rows, rows), jnp.float32),
        in_specs=[hbm, hbm, hbm, hbm],
        out_specs=vmem,
        scratch_shapes=[
            pltpu.VMEM((blocks, slots), jnp.int32),
            pltpu.VMEM((blocks, slots), jnp.int32),
            pltpu.VMEM((blocks, slots, rows, cols), jnp.int32),
            pltpu.VMEM((blocks, rows), jnp.int32),
            pltpu.VMEM((blocks, slots, rows, cols), jnp.bfloat16),
            pltpu.VMEM((n_doc, blocks + 1, table_rows, cols), jnp.float32),
            pltpu.VMEM((n_doc, per_core, slots, rows, cols), jnp.bfloat16),
            pltpu.VMEM((blocks, slots, rows, cols), jnp.bfloat16),
            pltpu.VMEM((slots, rows, cols), jnp.bfloat16),
            pltpu.VMEM((n_right, n_term, blocks, part_rows, rows), jnp.float32),
            pltpu.VMEM((n_right, n_term, blocks, part_rows, rows), jnp.int16),
            pltpu.VMEM((n_term, scale_rows, rows), jnp.float32),
            pltpu.VMEM((n_right, n_term, blocks, part_rows, rows), jnp.int16),
            pltpu.VMEM((n_term, scale_rows, rows), jnp.float32),
            pltpu.VMEM((square_rows, rows), jnp.float32),
            pltpu.VMEM((n_term, square_rows, rows), jnp.float32),
            pltpu.VMEM((rows, rows), jnp.float32),
            pltpu.VMEM((n_right, blocks, part_rows, rows), jnp.float32),
            pltpu.VMEM((n_pair, n_right, blocks, part_rows, rows), jnp.float32),
            dma((3 + blocks,)),
            dma((n_doc,)),
            dma((n_doc,)),
            dma((n_doc,)),
            dma((n_doc,)),
            dma((n_right, n_term)),
            dma((n_right, n_term)),
            dma((n_term,)),
            dma((n_term,)),
            dma((n_term,)),
            dma((n_term,)),
            dma((n_right, n_pair)),
            dma((n_right, n_pair)),
        ],
        compiler_params=pltpu.CompilerParams(
            collective_id=0, has_side_effects=True, vmem_limit_bytes=48 * 1024 * 1024
        ),
    )(*[pltpu.with_memory_space_constraint(x, pltpu.HBM) for x in (live_slots, block_ids, counts, lengths.reshape(blocks, rows))])
    return pl.pallas_call(
        functools.partial(place_kernel, sizes, blocks),
        out_shape=jax.ShapeDtypeStruct((pairs.shape[0], part_rows, rows), jnp.float32),
        in_specs=[smem, smem, pl.BlockSpec(memory_space=pl.ANY)],
        out_specs=hbm,
        scratch_shapes=[pltpu.SMEM((n_doc * blocks,), jnp.int32), dma(())],
        compiler_params=pltpu.CompilerParams(vmem_limit_bytes=48 * 1024 * 1024),
    )(pairs.T, pair_count, tiles)


def solution(mesh):
    sizes = (mesh.shape["doc"], mesh.shape["term"], mesh.shape["pair"])
    in_specs = (
        P("doc", "term", None, None),
        P("doc", "term"),
        P("doc", "term"),
        P("doc"),
        P(("doc", "pair"), None),
        P(("doc", "pair")),
    )
    out_specs = P(("doc", "pair"), "term", None)
    return jax.shard_map(
        functools.partial(shards, sizes),
        mesh=mesh,
        in_specs=in_specs,
        out_specs=out_specs,
        check_vma=False,
    )
```

```python
import functools

import jax
import jax.numpy as jnp
from jax import lax
from jax.experimental import pallas as pl
from jax.experimental.pallas import tpu as pltpu
from jax.sharding import PartitionSpec as P

steps = 32767.0
tiny = 1e-30
saturation = 1.2
length_weight = 0.75
epsilon = 1e-06

MESH = pl.DeviceIdType.MESH


def exclusive_or(a, b, count):
    result, bit = 0, 1
    while bit < count:
        x, y = lax.rem(a // bit, 2), lax.rem(b // bit, 2)
        result = result + bit * (x + y - 2 * x * y)
        bit *= 2
    return result


def target_of(me, k, count):
    if count & (count - 1):
        return lax.rem(me + k, count)
    return exclusive_or(me, k, count)


def slot_of(me, owner, count):
    if count & (count - 1):
        return lax.rem(me - owner + count, count)
    return exclusive_or(me, owner, count)


def tiles_kernel(
    sizes,
    live_hbm,
    ids_hbm,
    counts_hbm,
    lengths_hbm,
    out_ref,
    live_ref,
    ids_ref,
    counts_ref,
    lengths_ref,
    masked,
    small,
    right_counts,
    left_weight,
    right_weight,
    aligned,
    freq_table,
    length_table,
    partial_sum,
    coded,
    term_recv,
    side_own,
    side_recv,
    square_own,
    inverse_ref,
    column,
    final,
    pair_recv,
    load_sem,
    small_send_sem,
    small_recv_sem,
    count_send_sem,
    count_recv_sem,
    term_send_sem,
    term_recv_sem,
    side_send_sem,
    side_recv_sem,
    pair_send_sem,
    pair_recv_sem,
):
    n_doc, n_term, n_pair = sizes
    blocks, slots, rows, cols = counts_ref.shape
    per_core = blocks // n_pair
    n_right = n_doc * per_core
    part_rows = rows // n_term
    docs_all = n_doc * blocks * rows
    me_doc = lax.axis_index("doc")
    me_term = lax.axis_index("term")
    me_pair = lax.axis_index("pair")

    def doc_peer(k):
        return {"doc": target_of(me_doc, k, n_doc)}

    def term_peer(k):
        return {"term": lax.rem(me_term + k, n_term)}

    def pair_peer(k):
        return {"pair": lax.rem(me_pair + k, n_pair)}

    def small_copy(k):
        return pltpu.make_async_remote_copy(
            src_ref=small.at[0],
            dst_ref=small.at[k],
            send_sem=small_send_sem.at[k],
            recv_sem=small_recv_sem.at[k],
            device_id=doc_peer(k),
            device_id_type=MESH,
        )

    def count_copy(k):
        return pltpu.make_async_remote_copy(
            src_ref=masked.at[pl.ds(me_pair * per_core, per_core)],
            dst_ref=right_counts.at[k],
            send_sem=count_send_sem.at[k],
            recv_sem=count_recv_sem.at[k],
            device_id=doc_peer(k),
            device_id_type=MESH,
        )

    def term_copy(m, k):
        return pltpu.make_async_remote_copy(
            src_ref=coded.at[m, lax.rem(me_term + k, n_term)],
            dst_ref=term_recv.at[m, k],
            send_sem=term_send_sem.at[m, k],
            recv_sem=term_recv_sem.at[m, k],
            device_id=term_peer(k),
            device_id_type=MESH,
        )

    def side_copy(k):
        return pltpu.make_async_remote_copy(
            src_ref=side_own.at[lax.rem(me_term + k, n_term)],
            dst_ref=side_recv.at[k],
            send_sem=side_send_sem.at[k],
            recv_sem=side_recv_sem.at[k],
            device_id=term_peer(k),
            device_id_type=MESH,
        )

    def pair_copy(m, k):
        return pltpu.make_async_remote_copy(
            src_ref=final.at[m],
            dst_ref=pair_recv.at[k, m],
            send_sem=pair_send_sem.at[m, k],
            recv_sem=pair_recv_sem.at[m, k],
            device_id=pair_peer(k),
            device_id_type=MESH,
        )

    barrier = pltpu.get_barrier_semaphore()
    for k in range(1, n_doc):
        pl.semaphore_signal(barrier, inc=1, device_id=doc_peer(k), device_id_type=MESH)
    for k in range(1, n_term):
        pl.semaphore_signal(barrier, inc=1, device_id=term_peer(k), device_id_type=MESH)
    for k in range(1, n_pair):
        pl.semaphore_signal(barrier, inc=1, device_id=pair_peer(k), device_id_type=MESH)

    loads = [
        pltpu.make_async_copy(live_hbm, live_ref, load_sem.at[0]),
        pltpu.make_async_copy(ids_hbm, ids_ref, load_sem.at[1]),
        pltpu.make_async_copy(lengths_hbm, lengths_ref, load_sem.at[2]),
    ]
    loads += [
        pltpu.make_async_copy(counts_hbm.at[b], counts_ref.at[b], load_sem.at[3 + b])
        for b in range(blocks)
    ]
    for load in loads:
        load.start()
    small[0] = jnp.zeros(small.shape[1:], jnp.float32)
    square_own[...] = jnp.zeros(square_own.shape, jnp.float32)
    out_ref[out_ref.shape[0] - 1] = jnp.zeros(out_ref.shape[1:], jnp.float32)
    for load in loads[:3]:
        load.wait()
    for b in range(blocks):
        loads[3 + b].wait()
        for s in range(slots):
            live = jnp.broadcast_to(live_ref[b : b + 1, s : s + 1], (rows, cols)) > 0
            value = jnp.where(live, counts_ref[b, s].astype(jnp.float32), 0.0)
            masked[b, s] = value.astype(jnp.bfloat16)
            small[0, b, s : s + 1] = jnp.sum(
                jnp.where(value > 0.0, 1.0, 0.0), axis=0, keepdims=True
            )
            small[0, b, slots + s : slots + s + 1] = jnp.broadcast_to(
                ids_ref[b : b + 1, s : s + 1], (1, cols)
            ).astype(jnp.float32)
    small[0, blocks, 0:blocks] = lengths_ref[...].astype(jnp.float32)

    pl.semaphore_wait(barrier, n_doc + n_term + n_pair - 3)

    for k in range(1, n_doc):
        small_copy(k).start()
    first = [k for k in range(1, n_doc) if k & (k - 1) == 0]
    for k in first:
        count_copy(k).start()
    for k in range(1, n_doc):
        small_copy(k).wait_recv()

    total_len = lax.fori_loop(
        0,
        n_doc,
        lambda k, acc: acc + jnp.sum(small[k, blocks], axis=0, keepdims=True),
        jnp.zeros((1, cols), jnp.float32),
    )
    avg_len = jnp.sum(total_len, axis=1, keepdims=True) / docs_all

    def inv_freq_of(ids):
        def add(k, acc):
            for b in range(blocks):
                table = small[k, b]
                for s in range(slots):
                    same = ids == table[slots + s : slots + s + 1]
                    acc = acc + jnp.where(same, table[s : s + 1], 0.0)
            return acc

        freq = lax.fori_loop(
            0, n_doc, add, jnp.zeros(ids.shape, jnp.float32), unroll=min(n_doc, 4)
        )
        return jnp.log(1.0 + (docs_all - freq + 0.5) / (freq + 0.5))

    def prepare(k, b, place):
        freq_table[place] = inv_freq_of(small[k, b, slots : 2 * slots]) * (saturation + 1.0)
        length = small[k, blocks, pl.ds(b, 1)]
        scale = saturation * (1.0 - length_weight + length_weight * length / avg_len)
        length_table[place] = jnp.transpose(jnp.broadcast_to(scale, (rows, rows)))

    def weigh(read, target, place):
        squares = jnp.zeros((rows, cols), jnp.float32)
        for s in range(slots):
            freq = read(s).astype(jnp.float32)
            weight = freq_table[place, s : s + 1] * freq / (freq + length_table[place])
            squares = squares + weight * weight
            target[s] = weight.astype(jnp.bfloat16)
        return squares

    def keep_squares(squares, place):
        square_own[pl.ds(place, 1)] = jnp.sum(jnp.transpose(squares), axis=0, keepdims=True)

    def grams(m, right, right_ids):
        for b in range(blocks):
            left_ids = small[0, b, slots : 2 * slots]
            for j in range(slots):
                total = jnp.zeros((rows, cols), jnp.bfloat16)
                for i in range(slots):
                    same = left_ids[i : i + 1] == right_ids[j : j + 1]
                    same = jnp.where(same, 1.0, 0.0).astype(jnp.bfloat16)
                    total = total + left_weight[b, i] * same
                aligned[b * rows : (b + 1) * rows, j * cols : (j + 1) * cols] = total
        gram = lax.dot_general(
            aligned[...],
            jnp.concatenate([right[j] for j in range(slots)], axis=1),
            (((1,), (1,)), ((), ())),
            preferred_element_type=jnp.float32,
        )
        for z in range(n_term):
            for b in range(blocks):
                start = b * rows + z * part_rows
                piece = gram[start : start + part_rows]
                top = jnp.maximum(jnp.max(piece, axis=0, keepdims=True), tiny)
                partial_sum[m, z, b] = piece
                code = (piece * (steps / top) + 0.5).astype(jnp.int32)
                coded[m, z, b] = code.astype(jnp.int16)
                side_own[z, pl.ds(m * blocks + b, 1)] = top * (1.0 / steps)
        for k in range(1, n_term):
            term_copy(m, k).start()

    for b in range(blocks):
        prepare(0, b, b)
    left_squares = [
        weigh(lambda s, b=b: masked[b, s], left_weight.at[b], b) for b in range(blocks)
    ]
    for i in range(per_core):
        own = me_pair * per_core + i
        grams(i, left_weight.at[own], small[0, own, slots : 2 * slots])
    for k in range(1, n_doc):
        if k not in first:
            count_copy(k).start()
    for b in range(blocks):
        keep_squares(left_squares[b], b)
    for i in range(per_core):
        square_own[pl.ds(blocks + i, 1)] = square_own[pl.ds(me_pair * per_core + i, 1)]

    def prepare_right(k, carry):
        for i in range(per_core):
            prepare(k, me_pair * per_core + i, blocks + k * per_core + i)
        return carry

    lax.fori_loop(1, n_doc, prepare_right, 0)

    def right_step(k, carry):
        count_copy(k).wait_recv()
        for i in range(per_core):
            m = k * per_core + i
            squares = weigh(lambda s, i=i: right_counts[k, i, s], right_weight, blocks + m)
            grams(m, right_weight, small[k, me_pair * per_core + i, slots : 2 * slots])
            keep_squares(squares, blocks + m)
        return carry

    lax.fori_loop(1, n_doc, right_step, 0)

    scale_rows = side_own.shape[1] - square_own.shape[0]
    squares = square_own[...]
    for z in range(n_term):
        side_own[z, scale_rows:] = squares
    for k in range(1, n_term):
        side_copy(k).start()
    for k in range(1, n_term):
        side_copy(k).wait_recv()
        squares = squares + side_recv[k, scale_rows:]
    inverse = lax.rsqrt(squares + epsilon)
    inverse_ref[...] = inverse
    left_scale = []
    for b in range(blocks):
        column[...] = jnp.transpose(jnp.broadcast_to(inverse[b : b + 1], (rows, rows)))
        left_scale.append(column[pl.ds(me_term * part_rows, part_rows)])

    def finish(m, carry):
        for k in range(1, n_term):
            term_copy(m, k).wait_recv()
        right_scale = inverse_ref[pl.ds(blocks + m, 1)]
        for b in range(blocks):
            total = partial_sum[m, me_term, b]
            for k in range(1, n_term):
                scale = side_recv[k, pl.ds(m * blocks + b, 1)]
                total = total + term_recv[m, k, b].astype(jnp.float32) * scale
            value = total * left_scale[b] * right_scale
            final[m, b] = value
            out_ref[m * blocks + b] = value
        for k in range(1, n_pair):
            pair_copy(m, k).start()
        return carry

    lax.fori_loop(0, n_right, finish, 0)

    def collect(m, carry):
        for k in range(1, n_pair):
            pair_copy(m, k).wait_recv()
            out_ref[pl.ds((k * n_right + m) * blocks, blocks)] = pair_recv[k, m]
        for k in range(1, n_term):
            term_copy(m, k).wait_send()
        for k in range(1, n_pair):
            pair_copy(m, k).wait_send()
        return carry

    lax.fori_loop(0, n_right, collect, 0)
    for k in range(1, n_term):
        side_copy(k).wait_send()
    for k in range(1, n_doc):
        small_copy(k).wait_send()
        count_copy(k).wait_send()


def place_kernel(sizes, blocks, pairs_ref, count_ref, tiles_ref, out_ref, first_tile, sem):
    n_doc, n_term, n_pair = sizes
    per_core = blocks // n_pair
    n_right = n_doc * per_core
    me_doc = lax.axis_index("doc")
    me_pair = lax.axis_index("pair")
    count = count_ref[0]
    zero_tile = tiles_ref.shape[0] - 1

    def fill(owner, carry):
        k = slot_of(me_doc, owner, n_doc)
        for inner in range(blocks):
            side = lax.rem(me_pair - inner // per_core + n_pair, n_pair)
            m = side * n_right + k * per_core + inner % per_core
            first_tile[owner * blocks + inner] = (m - me_doc) * blocks
        return carry

    lax.fori_loop(0, n_doc, fill, 0)

    def step(row, carry):
        tile = first_tile[pairs_ref[1, row]] + pairs_ref[0, row]
        tile = jnp.where(row < count, tile, zero_tile)
        pltpu.make_async_copy(tiles_ref.at[tile], out_ref.at[row], sem).start()
        return carry

    lax.fori_loop(0, out_ref.shape[0], step, 0, unroll=8)
    pltpu.make_async_copy(out_ref, out_ref, sem).wait()


def shards(sizes, counts, block_ids, live_slots, lengths, pairs, pair_count):
    n_doc, n_term, n_pair = sizes
    blocks, slots, rows, cols = counts.shape
    per_core = blocks // n_pair
    n_right = n_doc * per_core
    part_rows = rows // n_term
    table_rows = -(-max(2 * slots, blocks) // 8) * 8
    square_rows = -(-(blocks + n_right) // 8) * 8
    dma = pltpu.SemaphoreType.DMA
    scale_rows = -(-(blocks * n_right) // 8) * 8
    hbm = pl.BlockSpec(memory_space=pltpu.HBM)
    smem = pl.BlockSpec(memory_space=pltpu.SMEM)
    vmem = pl.BlockSpec(memory_space=pltpu.VMEM)
    tiles = pl.pallas_call(
        functools.partial(tiles_kernel, sizes),
        out_shape=pltpu.VMEM((n_pair * n_right * blocks + 1, part_rows, rows), jnp.float32),
        in_specs=[hbm, hbm, hbm, hbm],
        out_specs=vmem,
        scratch_shapes=[
            pltpu.VMEM((blocks, slots), jnp.int32),
            pltpu.VMEM((blocks, slots), jnp.int32),
            pltpu.VMEM((blocks, slots, rows, cols), jnp.int32),
            pltpu.VMEM((blocks, rows), jnp.int32),
            pltpu.VMEM((blocks, slots, rows, cols), jnp.bfloat16),
            pltpu.VMEM((n_doc, blocks + 1, table_rows, cols), jnp.float32),
            pltpu.VMEM((n_doc, per_core, slots, rows, cols), jnp.bfloat16),
            pltpu.VMEM((blocks, slots, rows, cols), jnp.bfloat16),
            pltpu.VMEM((slots, rows, cols), jnp.bfloat16),
            pltpu.VMEM((blocks * rows, slots * cols), jnp.bfloat16),
            pltpu.VMEM((blocks + n_right, slots, cols), jnp.float32),
            pltpu.VMEM((blocks + n_right, rows, rows), jnp.float32),
            pltpu.VMEM((n_right, n_term, blocks, part_rows, rows), jnp.float32),
            pltpu.VMEM((n_right, n_term, blocks, part_rows, rows), jnp.int16),
            pltpu.VMEM((n_right, n_term, blocks, part_rows, rows), jnp.int16),
            pltpu.VMEM((n_term, scale_rows + square_rows, rows), jnp.float32),
            pltpu.VMEM((n_term, scale_rows + square_rows, rows), jnp.float32),
            pltpu.VMEM((square_rows, rows), jnp.float32),
            pltpu.VMEM((square_rows, rows), jnp.float32),
            pltpu.VMEM((rows, rows), jnp.float32),
            pltpu.VMEM((n_right, blocks, part_rows, rows), jnp.float32),
            pltpu.VMEM((n_pair, n_right, blocks, part_rows, rows), jnp.float32),
            dma((3 + blocks,)),
            dma((n_doc,)),
            dma((n_doc,)),
            dma((n_doc,)),
            dma((n_doc,)),
            dma((n_right, n_term)),
            dma((n_right, n_term)),
            dma((n_term,)),
            dma((n_term,)),
            dma((n_right, n_pair)),
            dma((n_right, n_pair)),
        ],
        compiler_params=pltpu.CompilerParams(
            collective_id=0, has_side_effects=True, vmem_limit_bytes=48 * 1024 * 1024
        ),
    )(*[pltpu.with_memory_space_constraint(x, pltpu.HBM) for x in (live_slots, block_ids, counts, lengths.reshape(blocks, rows))])
    return pl.pallas_call(
        functools.partial(place_kernel, sizes, blocks),
        out_shape=jax.ShapeDtypeStruct((pairs.shape[0], part_rows, rows), jnp.float32),
        in_specs=[smem, smem, pl.BlockSpec(memory_space=pl.ANY)],
        out_specs=hbm,
        scratch_shapes=[pltpu.SMEM((n_doc * blocks,), jnp.int32), dma(())],
        compiler_params=pltpu.CompilerParams(vmem_limit_bytes=48 * 1024 * 1024),
    )(pairs.T, pair_count, tiles)


def solution(mesh):
    sizes = (mesh.shape["doc"], mesh.shape["term"], mesh.shape["pair"])
    in_specs = (
        P("doc", "term", None, None),
        P("doc", "term"),
        P("doc", "term"),
        P("doc"),
        P(("doc", "pair"), None),
        P(("doc", "pair")),
    )
    out_specs = P(("doc", "pair"), "term", None)
    return jax.shard_map(
        functools.partial(shards, sizes),
        mesh=mesh,
        in_specs=in_specs,
        out_specs=out_specs,
        check_vma=False,
    )
```

```python
import functools

import jax
import jax.numpy as jnp
from jax import lax
from jax.experimental import pallas as pl
from jax.experimental.pallas import tpu as pltpu
from jax.sharding import PartitionSpec as P

steps = 32767.0
tiny = 1e-30
saturation = 1.2
length_weight = 0.75
epsilon = 1e-06

MESH = pl.DeviceIdType.MESH


def exclusive_or(a, b, count):
    result, bit = 0, 1
    while bit < count:
        x, y = lax.rem(a // bit, 2), lax.rem(b // bit, 2)
        result = result + bit * (x + y - 2 * x * y)
        bit *= 2
    return result


def target_of(me, k, count):
    if count & (count - 1):
        return lax.rem(me + k, count)
    return exclusive_or(me, k, count)


def slot_of(me, owner, count):
    if count & (count - 1):
        return lax.rem(me - owner + count, count)
    return exclusive_or(me, owner, count)


def tiles_kernel(
    sizes,
    live_hbm,
    ids_hbm,
    counts_hbm,
    lengths_hbm,
    out_ref,
    live_ref,
    ids_ref,
    counts_ref,
    lengths_ref,
    masked,
    small,
    right_counts,
    left_weight,
    right_weight,
    aligned,
    ids_table,
    freq_table,
    length_table,
    partial_sum,
    coded,
    term_recv,
    side_own,
    side_recv,
    square_own,
    inverse_ref,
    final,
    pair_recv,
    load_sem,
    small_send_sem,
    small_recv_sem,
    count_send_sem,
    count_recv_sem,
    term_send_sem,
    term_recv_sem,
    side_send_sem,
    side_recv_sem,
    pair_send_sem,
    pair_recv_sem,
):
    n_doc, n_term, n_pair = sizes
    blocks, slots, rows, cols = counts_ref.shape
    per_core = blocks // n_pair
    n_right = n_doc * per_core
    part_rows = rows // n_term
    docs_all = n_doc * blocks * rows
    me_doc = lax.axis_index("doc")
    me_term = lax.axis_index("term")
    me_pair = lax.axis_index("pair")

    def doc_peer(k):
        return {"doc": target_of(me_doc, k, n_doc)}

    def term_peer(k):
        return {"term": lax.rem(me_term + k, n_term)}

    def pair_peer(k):
        return {"pair": lax.rem(me_pair + k, n_pair)}

    def small_copy(k):
        return pltpu.make_async_remote_copy(
            src_ref=small.at[0],
            dst_ref=small.at[k],
            send_sem=small_send_sem.at[k],
            recv_sem=small_recv_sem.at[k],
            device_id=doc_peer(k),
            device_id_type=MESH,
        )

    def count_copy(k):
        return pltpu.make_async_remote_copy(
            src_ref=masked.at[pl.ds(me_pair * per_core, per_core)],
            dst_ref=right_counts.at[k],
            send_sem=count_send_sem.at[k],
            recv_sem=count_recv_sem.at[k],
            device_id=doc_peer(k),
            device_id_type=MESH,
        )

    def term_copy(m, k):
        return pltpu.make_async_remote_copy(
            src_ref=coded.at[m, lax.rem(me_term + k, n_term)],
            dst_ref=term_recv.at[m, k],
            send_sem=term_send_sem.at[m, k],
            recv_sem=term_recv_sem.at[m, k],
            device_id=term_peer(k),
            device_id_type=MESH,
        )

    def side_copy(k):
        return pltpu.make_async_remote_copy(
            src_ref=side_own.at[lax.rem(me_term + k, n_term)],
            dst_ref=side_recv.at[k],
            send_sem=side_send_sem.at[k],
            recv_sem=side_recv_sem.at[k],
            device_id=term_peer(k),
            device_id_type=MESH,
        )

    def pair_copy(m, k):
        return pltpu.make_async_remote_copy(
            src_ref=final.at[m],
            dst_ref=pair_recv.at[k, m],
            send_sem=pair_send_sem.at[m, k],
            recv_sem=pair_recv_sem.at[m, k],
            device_id=pair_peer(k),
            device_id_type=MESH,
        )

    barrier = pltpu.get_barrier_semaphore()
    for k in range(1, n_doc):
        pl.semaphore_signal(barrier, inc=1, device_id=doc_peer(k), device_id_type=MESH)
    for k in range(1, n_term):
        pl.semaphore_signal(barrier, inc=1, device_id=term_peer(k), device_id_type=MESH)
    for k in range(1, n_pair):
        pl.semaphore_signal(barrier, inc=1, device_id=pair_peer(k), device_id_type=MESH)

    loads = [
        pltpu.make_async_copy(live_hbm, live_ref, load_sem.at[0]),
        pltpu.make_async_copy(ids_hbm, ids_ref, load_sem.at[1]),
        pltpu.make_async_copy(lengths_hbm, lengths_ref, load_sem.at[2]),
    ]
    loads += [
        pltpu.make_async_copy(counts_hbm.at[b], counts_ref.at[b], load_sem.at[3 + b])
        for b in range(blocks)
    ]
    for load in loads:
        load.start()
    small[0] = jnp.zeros(small.shape[1:], jnp.float32)
    square_own[...] = jnp.zeros(square_own.shape, jnp.float32)
    out_ref[out_ref.shape[0] - 1] = jnp.zeros(out_ref.shape[1:], jnp.float32)
    for load in loads[:3]:
        load.wait()
    for b in range(blocks):
        loads[3 + b].wait()
        for s in range(slots):
            live = jnp.broadcast_to(live_ref[b : b + 1, s : s + 1], (rows, cols)) > 0
            value = jnp.where(live, counts_ref[b, s].astype(jnp.float32), 0.0)
            masked[b, s] = value.astype(jnp.bfloat16)
            small[0, b, s : s + 1] = jnp.sum(
                jnp.where(value > 0.0, 1.0, 0.0), axis=0, keepdims=True
            )
            small[0, b, slots + s : slots + s + 1] = jnp.broadcast_to(
                ids_ref[b : b + 1, s : s + 1], (1, cols)
            ).astype(jnp.float32)
    small[0, blocks, 0:blocks] = lengths_ref[...].astype(jnp.float32)

    pl.semaphore_wait(barrier, n_doc + n_term + n_pair - 3)

    for k in range(1, n_doc):
        small_copy(k).start()
    for k in sorted(range(1, n_doc), key=lambda k: k & (k - 1) != 0):
        count_copy(k).start()
    for k in range(1, n_doc):
        small_copy(k).wait_recv()

    row_at = lax.broadcasted_iota(jnp.int32, (rows, cols), 0)
    col_at = lax.broadcasted_iota(jnp.int32, (rows, cols), 1)
    diagonal = row_at == col_at
    part_diagonal = row_at[:part_rows] + me_term * part_rows == col_at[:part_rows]
    total_len = lax.fori_loop(
        0,
        n_doc,
        lambda k, acc: acc + jnp.sum(small[k, blocks], axis=0, keepdims=True),
        jnp.zeros((1, cols), jnp.float32),
    )
    avg_len = jnp.sum(total_len, axis=1, keepdims=True) / docs_all

    def table_row(k, b, place):
        ids_table[pl.ds(place * slots, slots)] = small[k, b, slots : 2 * slots]
        length = small[k, blocks, pl.ds(b, 1)]
        scale = saturation * (1.0 - length_weight + length_weight * length / avg_len)
        scale = jnp.sum(jnp.where(diagonal, scale, 0.0), axis=1, keepdims=True)
        length_table[place] = jnp.broadcast_to(scale, (rows, cols))

    for b in range(blocks):
        table_row(0, b, b)

    def right_rows(k, carry):
        for i in range(per_core):
            table_row(k, me_pair * per_core + i, blocks + k * per_core + i)
        return carry

    lax.fori_loop(0, n_doc, right_rows, 0, unroll=min(n_doc, 4))
    ids = ids_table[...]

    def add(k, acc):
        for b in range(blocks):
            table = small[k, b]
            for s in range(slots):
                same = ids == table[slots + s : slots + s + 1]
                acc = acc + jnp.where(same, table[s : s + 1], 0.0)
        return acc

    doc_freq = lax.fori_loop(
        0, n_doc, add, jnp.zeros(ids.shape, jnp.float32), unroll=min(n_doc, 4)
    )
    freq_table[...] = jnp.log(1.0 + (docs_all - doc_freq + 0.5) / (doc_freq + 0.5)) * (
        saturation + 1.0
    )

    def weigh(read, target, place):
        squares = jnp.zeros((rows, cols), jnp.float32)
        for s in range(slots):
            freq = read(s).astype(jnp.float32)
            weight = freq_table[pl.ds(place * slots + s, 1)] * freq / (freq + length_table[place])
            squares = squares + weight * weight
            target[s] = weight.astype(jnp.bfloat16)
        return squares

    def keep_squares(squares, place):
        squares = jnp.sum(squares, axis=1, keepdims=True)
        squares = jnp.where(diagonal, squares, 0.0)
        square_own[pl.ds(place, 1)] = jnp.sum(squares, axis=0, keepdims=True)

    def grams(m, right, right_ids):
        for b in range(blocks):
            left_ids = small[0, b, slots : 2 * slots]
            for j in range(slots):
                total = jnp.zeros((rows, cols), jnp.bfloat16)
                for i in range(slots):
                    same = left_ids[i : i + 1] == right_ids[j : j + 1]
                    same = jnp.where(same, 1.0, 0.0).astype(jnp.bfloat16)
                    total = total + left_weight[b, i] * same
                aligned[b * rows : (b + 1) * rows, j * cols : (j + 1) * cols] = total
        gram = lax.dot_general(
            aligned[...],
            jnp.concatenate([right[j] for j in range(slots)], axis=1),
            (((1,), (1,)), ((), ())),
            preferred_element_type=jnp.float32,
        )
        for z in range(n_term):
            for b in range(blocks):
                start = b * rows + z * part_rows
                piece = gram[start : start + part_rows]
                top = jnp.maximum(jnp.max(piece, axis=0, keepdims=True), tiny)
                partial_sum[m, z, b] = piece
                code = (piece * (steps / top) + 0.5).astype(jnp.int32)
                coded[m, z, b] = code.astype(jnp.int16)
                side_own[z, pl.ds(m * blocks + b, 1)] = top * (1.0 / steps)
        for k in range(1, n_term):
            term_copy(m, k).start()

    left_squares = [
        weigh(lambda s, b=b: masked[b, s], left_weight.at[b], b) for b in range(blocks)
    ]
    for i in range(per_core):
        own = me_pair * per_core + i
        grams(i, left_weight.at[own], small[0, own, slots : 2 * slots])
    for b in range(blocks):
        keep_squares(left_squares[b], b)
    for i in range(per_core):
        square_own[pl.ds(blocks + i, 1)] = square_own[pl.ds(me_pair * per_core + i, 1)]

    def right_step(k, carry):
        count_copy(k).wait_recv()
        for i in range(per_core):
            m = k * per_core + i
            squares = weigh(lambda s, i=i: right_counts[k, i, s], right_weight, blocks + m)
            grams(m, right_weight, small[k, me_pair * per_core + i, slots : 2 * slots])
            keep_squares(squares, blocks + m)
        return carry

    lax.fori_loop(1, n_doc, right_step, 0)

    scale_rows = side_own.shape[1] - square_own.shape[0]
    squares = square_own[...]
    for z in range(n_term):
        side_own[z, scale_rows:] = squares
    for k in range(1, n_term):
        side_copy(k).start()
    for k in range(1, n_term):
        side_copy(k).wait_recv()
        squares = squares + side_recv[k, scale_rows:]
    inverse = lax.rsqrt(squares + epsilon)
    inverse_ref[...] = inverse
    left_scale = []
    for b in range(blocks):
        picked = jnp.where(part_diagonal, inverse[b : b + 1], 0.0)
        left_scale.append(jnp.sum(picked, axis=1, keepdims=True))

    def finish(m, carry):
        for k in range(1, n_term):
            term_copy(m, k).wait_recv()
        right_scale = inverse_ref[pl.ds(blocks + m, 1)]
        for b in range(blocks):
            total = partial_sum[m, me_term, b]
            for k in range(1, n_term):
                scale = side_recv[k, pl.ds(m * blocks + b, 1)]
                total = total + term_recv[m, k, b].astype(jnp.float32) * scale
            value = total * left_scale[b] * right_scale
            final[m, b] = value
            out_ref[m * blocks + b] = value
        for k in range(1, n_pair):
            pair_copy(m, k).start()
        return carry

    lax.fori_loop(0, n_right, finish, 0)

    def collect(m, carry):
        for k in range(1, n_pair):
            pair_copy(m, k).wait_recv()
            out_ref[pl.ds((k * n_right + m) * blocks, blocks)] = pair_recv[k, m]
        for k in range(1, n_term):
            term_copy(m, k).wait_send()
        for k in range(1, n_pair):
            pair_copy(m, k).wait_send()
        return carry

    lax.fori_loop(0, n_right, collect, 0)
    for k in range(1, n_term):
        side_copy(k).wait_send()
    for k in range(1, n_doc):
        small_copy(k).wait_send()
        count_copy(k).wait_send()


def place_kernel(sizes, blocks, pairs_ref, count_ref, tiles_ref, out_ref, first_tile, sem):
    n_doc, n_term, n_pair = sizes
    per_core = blocks // n_pair
    n_right = n_doc * per_core
    me_doc = lax.axis_index("doc")
    me_pair = lax.axis_index("pair")
    count = count_ref[0]
    zero_tile = tiles_ref.shape[0] - 1

    def fill(owner, carry):
        k = slot_of(me_doc, owner, n_doc)
        for inner in range(blocks):
            side = lax.rem(me_pair - inner // per_core + n_pair, n_pair)
            m = side * n_right + k * per_core + inner % per_core
            first_tile[owner * blocks + inner] = (m - me_doc) * blocks
        return carry

    lax.fori_loop(0, n_doc, fill, 0)

    def step(row, carry):
        tile = first_tile[pairs_ref[1, row]] + pairs_ref[0, row]
        tile = jnp.where(row < count, tile, zero_tile)
        pltpu.make_async_copy(tiles_ref.at[tile], out_ref.at[row], sem).start()
        return carry

    lax.fori_loop(0, out_ref.shape[0], step, 0, unroll=8)
    pltpu.make_async_copy(out_ref, out_ref, sem).wait()


def shards(sizes, counts, block_ids, live_slots, lengths, pairs, pair_count):
    n_doc, n_term, n_pair = sizes
    blocks, slots, rows, cols = counts.shape
    per_core = blocks // n_pair
    n_right = n_doc * per_core
    part_rows = rows // n_term
    table_rows = -(-max(2 * slots, blocks) // 8) * 8
    square_rows = -(-(blocks + n_right) // 8) * 8
    dma = pltpu.SemaphoreType.DMA
    scale_rows = -(-(blocks * n_right) // 8) * 8
    hbm = pl.BlockSpec(memory_space=pltpu.HBM)
    smem = pl.BlockSpec(memory_space=pltpu.SMEM)
    vmem = pl.BlockSpec(memory_space=pltpu.VMEM)
    tiles = pl.pallas_call(
        functools.partial(tiles_kernel, sizes),
        out_shape=pltpu.VMEM((n_pair * n_right * blocks + 1, part_rows, rows), jnp.float32),
        in_specs=[hbm, hbm, hbm, hbm],
        out_specs=vmem,
        scratch_shapes=[
            pltpu.VMEM((blocks, slots), jnp.int32),
            pltpu.VMEM((blocks, slots), jnp.int32),
            pltpu.VMEM((blocks, slots, rows, cols), jnp.int32),
            pltpu.VMEM((blocks, rows), jnp.int32),
            pltpu.VMEM((blocks, slots, rows, cols), jnp.bfloat16),
            pltpu.VMEM((n_doc, blocks + 1, table_rows, cols), jnp.float32),
            pltpu.VMEM((n_doc, per_core, slots, rows, cols), jnp.bfloat16),
            pltpu.VMEM((blocks, slots, rows, cols), jnp.bfloat16),
            pltpu.VMEM((slots, rows, cols), jnp.bfloat16),
            pltpu.VMEM((blocks * rows, slots * cols), jnp.bfloat16),
            pltpu.VMEM(((blocks + n_right) * slots, cols), jnp.float32),
            pltpu.VMEM(((blocks + n_right) * slots, cols), jnp.float32),
            pltpu.VMEM((blocks + n_right, rows, rows), jnp.float32),
            pltpu.VMEM((n_right, n_term, blocks, part_rows, rows), jnp.float32),
            pltpu.VMEM((n_right, n_term, blocks, part_rows, rows), jnp.int16),
            pltpu.VMEM((n_right, n_term, blocks, part_rows, rows), jnp.int16),
            pltpu.VMEM((n_term, scale_rows + square_rows, rows), jnp.float32),
            pltpu.VMEM((n_term, scale_rows + square_rows, rows), jnp.float32),
            pltpu.VMEM((square_rows, rows), jnp.float32),
            pltpu.VMEM((square_rows, rows), jnp.float32),
            pltpu.VMEM((n_right, blocks, part_rows, rows), jnp.float32),
            pltpu.VMEM((n_pair, n_right, blocks, part_rows, rows), jnp.float32),
            dma((3 + blocks,)),
            dma((n_doc,)),
            dma((n_doc,)),
            dma((n_doc,)),
            dma((n_doc,)),
            dma((n_right, n_term)),
            dma((n_right, n_term)),
            dma((n_term,)),
            dma((n_term,)),
            dma((n_right, n_pair)),
            dma((n_right, n_pair)),
        ],
        compiler_params=pltpu.CompilerParams(
            collective_id=0, has_side_effects=True, vmem_limit_bytes=48 * 1024 * 1024
        ),
    )(*[pltpu.with_memory_space_constraint(x, pltpu.HBM) for x in (live_slots, block_ids, counts, lengths.reshape(blocks, rows))])
    return pl.pallas_call(
        functools.partial(place_kernel, sizes, blocks),
        out_shape=jax.ShapeDtypeStruct((pairs.shape[0], part_rows, rows), jnp.float32),
        in_specs=[smem, smem, pl.BlockSpec(memory_space=pl.ANY)],
        out_specs=hbm,
        scratch_shapes=[pltpu.SMEM((n_doc * blocks,), jnp.int32), dma(())],
        compiler_params=pltpu.CompilerParams(vmem_limit_bytes=48 * 1024 * 1024),
    )(pairs.T, pair_count, tiles)


def solution(mesh):
    sizes = (mesh.shape["doc"], mesh.shape["term"], mesh.shape["pair"])
    in_specs = (
        P("doc", "term", None, None),
        P("doc", "term"),
        P("doc", "term"),
        P("doc"),
        P(("doc", "pair"), None),
        P(("doc", "pair")),
    )
    out_specs = P(("doc", "pair"), "term", None)
    return jax.shard_map(
        functools.partial(shards, sizes),
        mesh=mesh,
        in_specs=in_specs,
        out_specs=out_specs,
        check_vma=False,
    )
```

```python
import functools

import jax
import jax.numpy as jnp
from jax import lax
from jax.experimental import pallas as pl
from jax.experimental.pallas import tpu as pltpu
from jax.sharding import PartitionSpec as P

steps = 32767.0
tiny = 1e-30
saturation = 1.2
length_weight = 0.75
epsilon = 1e-06

MESH = pl.DeviceIdType.MESH


def exclusive_or(a, b, count):
    result, bit = 0, 1
    while bit < count:
        x, y = lax.rem(a // bit, 2), lax.rem(b // bit, 2)
        result = result + bit * (x + y - 2 * x * y)
        bit *= 2
    return result


def target_of(me, k, count):
    if count & (count - 1):
        return lax.rem(me + k, count)
    return exclusive_or(me, k, count)


def slot_of(me, owner, count):
    if count & (count - 1):
        return lax.rem(me - owner + count, count)
    return exclusive_or(me, owner, count)


def tiles_kernel(
    sizes,
    live_hbm,
    ids_hbm,
    counts_hbm,
    lengths_hbm,
    pairs_hbm,
    limit_ref,
    out_ref,
    tile_ref,
    live_ref,
    ids_ref,
    counts_ref,
    lengths_ref,
    pairs_ref,
    number_ref,
    masked,
    small,
    right_counts,
    left_weight,
    right_weight,
    aligned,
    ids_table,
    freq_table,
    length_table,
    partial_sum,
    coded,
    term_recv,
    side_own,
    side_recv,
    square_own,
    inverse_ref,
    final,
    pair_recv,
    load_sem,
    small_send_sem,
    small_recv_sem,
    count_send_sem,
    count_recv_sem,
    term_send_sem,
    term_recv_sem,
    side_send_sem,
    side_recv_sem,
    pair_send_sem,
    pair_recv_sem,
):
    n_doc, n_term, n_pair = sizes
    blocks, slots, rows, cols = counts_ref.shape
    per_core = blocks // n_pair
    n_right = n_doc * per_core
    part_rows = rows // n_term
    docs_all = n_doc * blocks * rows
    me_doc = lax.axis_index("doc")
    me_term = lax.axis_index("term")
    me_pair = lax.axis_index("pair")

    def doc_peer(k):
        return {"doc": target_of(me_doc, k, n_doc)}

    def term_peer(k):
        return {"term": lax.rem(me_term + k, n_term)}

    def pair_peer(k):
        return {"pair": lax.rem(me_pair + k, n_pair)}

    def small_copy(k):
        return pltpu.make_async_remote_copy(
            src_ref=small.at[0],
            dst_ref=small.at[k],
            send_sem=small_send_sem.at[k],
            recv_sem=small_recv_sem.at[k],
            device_id=doc_peer(k),
            device_id_type=MESH,
        )

    def count_copy(k):
        return pltpu.make_async_remote_copy(
            src_ref=masked.at[pl.ds(me_pair * per_core, per_core)],
            dst_ref=right_counts.at[k],
            send_sem=count_send_sem.at[k],
            recv_sem=count_recv_sem.at[k],
            device_id=doc_peer(k),
            device_id_type=MESH,
        )

    relay = n_doc == 4
    near = 1 + lax.rem(me_pair, 2)
    far = 3 - near

    def relay_copy():
        return pltpu.make_async_remote_copy(
            src_ref=right_counts.at[near],
            dst_ref=right_counts.at[3],
            send_sem=count_send_sem.at[3],
            recv_sem=count_recv_sem.at[3],
            device_id=doc_peer(far),
            device_id_type=MESH,
        )

    def term_copy(m, k):
        return pltpu.make_async_remote_copy(
            src_ref=coded.at[m, lax.rem(me_term + k, n_term)],
            dst_ref=term_recv.at[m, k],
            send_sem=term_send_sem.at[m, k],
            recv_sem=term_recv_sem.at[m, k],
            device_id=term_peer(k),
            device_id_type=MESH,
        )

    def side_copy(k):
        return pltpu.make_async_remote_copy(
            src_ref=side_own.at[lax.rem(me_term + k, n_term)],
            dst_ref=side_recv.at[k],
            send_sem=side_send_sem.at[k],
            recv_sem=side_recv_sem.at[k],
            device_id=term_peer(k),
            device_id_type=MESH,
        )

    def pair_copy(m, k):
        return pltpu.make_async_remote_copy(
            src_ref=final.at[m],
            dst_ref=pair_recv.at[k, m],
            send_sem=pair_send_sem.at[m, k],
            recv_sem=pair_recv_sem.at[m, k],
            device_id=pair_peer(k),
            device_id_type=MESH,
        )

    barrier = pltpu.get_barrier_semaphore()
    for k in range(1, n_doc):
        pl.semaphore_signal(barrier, inc=1, device_id=doc_peer(k), device_id_type=MESH)
    for k in range(1, n_term):
        pl.semaphore_signal(barrier, inc=1, device_id=term_peer(k), device_id_type=MESH)
    for k in range(1, n_pair):
        pl.semaphore_signal(barrier, inc=1, device_id=pair_peer(k), device_id_type=MESH)

    loads = [
        pltpu.make_async_copy(live_hbm, live_ref, load_sem.at[0]),
        pltpu.make_async_copy(ids_hbm, ids_ref, load_sem.at[1]),
        pltpu.make_async_copy(lengths_hbm, lengths_ref, load_sem.at[2]),
    ]
    extra = [pltpu.make_async_copy(pairs_hbm, pairs_ref, load_sem.at[3 + blocks])]
    loads += [
        pltpu.make_async_copy(counts_hbm.at[b], counts_ref.at[b], load_sem.at[3 + b])
        for b in range(blocks)
    ]
    for load in loads + extra:
        load.start()
    small[0] = jnp.zeros(small.shape[1:], jnp.float32)
    square_own[...] = jnp.zeros(square_own.shape, jnp.float32)
    out_ref[out_ref.shape[0] - 1] = jnp.zeros(out_ref.shape[1:], jnp.float32)
    for load in loads[:3]:
        load.wait()
    for b in range(blocks):
        loads[3 + b].wait()
        for s in range(slots):
            live = jnp.broadcast_to(live_ref[b : b + 1, s : s + 1], (rows, cols)) > 0
            value = jnp.where(live, counts_ref[b, s].astype(jnp.float32), 0.0)
            masked[b, s] = value.astype(jnp.bfloat16)
            small[0, b, s : s + 1] = jnp.sum(
                jnp.where(value > 0.0, 1.0, 0.0), axis=0, keepdims=True
            )
            small[0, b, slots + s : slots + s + 1] = jnp.broadcast_to(
                ids_ref[b : b + 1, s : s + 1], (1, cols)
            ).astype(jnp.float32)
    small[0, blocks, 0:blocks] = lengths_ref[...].astype(jnp.float32)

    pl.semaphore_wait(barrier, n_doc + n_term + n_pair - 3)

    for k in range(1, n_doc):
        small_copy(k).start()
    for k in (near, far) if relay else range(1, n_doc):
        count_copy(k).start()
    for k in range(1, n_doc):
        small_copy(k).wait_recv()

    row_at = lax.broadcasted_iota(jnp.int32, (rows, cols), 0)
    col_at = lax.broadcasted_iota(jnp.int32, (rows, cols), 1)
    diagonal = row_at == col_at
    part_diagonal = row_at[:part_rows] + me_term * part_rows == col_at[:part_rows]
    total_len = lax.fori_loop(
        0,
        n_doc,
        lambda k, acc: acc + jnp.sum(small[k, blocks], axis=0, keepdims=True),
        jnp.zeros((1, cols), jnp.float32),
    )
    avg_len = jnp.sum(total_len, axis=1, keepdims=True) / docs_all

    def table_row(k, b, place):
        ids_table[pl.ds(place * slots, slots)] = small[k, b, slots : 2 * slots]
        length = small[k, blocks, pl.ds(b, 1)]
        scale = saturation * (1.0 - length_weight + length_weight * length / avg_len)
        scale = jnp.sum(jnp.where(diagonal, scale, 0.0), axis=1, keepdims=True)
        length_table[place] = jnp.broadcast_to(scale, (rows, cols))

    for b in range(blocks):
        table_row(0, b, b)

    def right_rows(k, carry):
        for i in range(per_core):
            table_row(k, me_pair * per_core + i, blocks + k * per_core + i)
        return carry

    lax.fori_loop(0, n_doc, right_rows, 0, unroll=min(n_doc, 4))
    ids = ids_table[...]

    def add(k, acc):
        for b in range(blocks):
            table = small[k, b]
            for s in range(slots):
                same = ids == table[slots + s : slots + s + 1]
                acc = acc + jnp.where(same, table[s : s + 1], 0.0)
        return acc

    doc_freq = lax.fori_loop(
        0, n_doc, add, jnp.zeros(ids.shape, jnp.float32), unroll=min(n_doc, 4)
    )
    freq_table[...] = jnp.log(1.0 + (docs_all - doc_freq + 0.5) / (doc_freq + 0.5)) * (
        saturation + 1.0
    )

    def weigh(read, target, place):
        squares = jnp.zeros((rows, cols), jnp.float32)
        for s in range(slots):
            freq = read(s).astype(jnp.float32)
            weight = freq_table[pl.ds(place * slots + s, 1)] * freq / (freq + length_table[place])
            squares = squares + weight * weight
            target[s] = weight.astype(jnp.bfloat16)
        return squares

    def keep_squares(squares, place):
        squares = jnp.sum(squares, axis=1, keepdims=True)
        squares = jnp.where(diagonal, squares, 0.0)
        square_own[pl.ds(place, 1)] = jnp.sum(squares, axis=0, keepdims=True)

    def grams(m, right, right_ids):
        for b in range(blocks):
            left_ids = small[0, b, slots : 2 * slots]
            for j in range(slots):
                total = jnp.zeros((rows, cols), jnp.bfloat16)
                for i in range(slots):
                    same = left_ids[i : i + 1] == right_ids[j : j + 1]
                    same = jnp.where(same, 1.0, 0.0).astype(jnp.bfloat16)
                    total = total + left_weight[b, i] * same
                aligned[b * rows : (b + 1) * rows, j * cols : (j + 1) * cols] = total
        gram = lax.dot_general(
            aligned[...],
            jnp.concatenate([right[j] for j in range(slots)], axis=1),
            (((1,), (1,)), ((), ())),
            preferred_element_type=jnp.float32,
        )
        for z in range(n_term):
            for b in range(blocks):
                start = b * rows + z * part_rows
                piece = gram[start : start + part_rows]
                top = jnp.maximum(jnp.max(piece, axis=0, keepdims=True), tiny)
                partial_sum[m, z, b] = piece
                code = (piece * (steps / top) + 0.5).astype(jnp.int32)
                coded[m, z, b] = code.astype(jnp.int16)
                side_own[z, pl.ds(m * blocks + b, 1)] = top * (1.0 / steps)
        for k in range(1, n_term):
            term_copy(m, k).start()

    left_squares = [
        weigh(lambda s, b=b: masked[b, s], left_weight.at[b], b) for b in range(blocks)
    ]
    for load in extra:
        load.wait()
    left = pairs_ref[0:1]
    right = pairs_ref[1:2]
    number = left - me_doc * blocks
    for block in range(n_doc * blocks):
        owner, inner = block // blocks, block % blocks
        side = lax.rem(me_pair - inner // per_core + n_pair, n_pair)
        m = slot_of(me_doc, owner, n_doc) * per_core + inner % per_core
        number = number + jnp.where(right == block, (side * n_right + m) * blocks, 0)
    row = lax.broadcasted_iota(jnp.int32, number.shape, 1)
    number_ref[...] = jnp.where(row < limit_ref[0], number, out_ref.shape[0] - 1)
    number_copy = pltpu.make_async_copy(number_ref, tile_ref, load_sem.at[4 + blocks])
    number_copy.start()

    if relay:
        count_copy(near).wait_recv()
        relay_copy().start()
    for i in range(per_core):
        own = me_pair * per_core + i
        grams(i, left_weight.at[own], small[0, own, slots : 2 * slots])
    for b in range(blocks):
        keep_squares(left_squares[b], b)
    for i in range(per_core):
        square_own[pl.ds(blocks + i, 1)] = square_own[pl.ds(me_pair * per_core + i, 1)]

    def right_step(step, carry):
        if relay:
            k = jnp.where(step == 1, near, jnp.where(step == 2, far, 3))

            @pl.when(step == 2)
            def _():
                count_copy(far).wait_recv()

            @pl.when(step == 3)
            def _():
                relay_copy().wait_recv()
        else:
            k = step
            count_copy(k).wait_recv()
        for i in range(per_core):
            m = k * per_core + i
            squares = weigh(lambda s, i=i: right_counts[k, i, s], right_weight, blocks + m)
            grams(m, right_weight, small[k, me_pair * per_core + i, slots : 2 * slots])
            keep_squares(squares, blocks + m)
        return carry

    lax.fori_loop(1, n_doc, right_step, 0)

    scale_rows = side_own.shape[1] - square_own.shape[0]
    squares = square_own[...]
    for z in range(n_term):
        side_own[z, scale_rows:] = squares
    for k in range(1, n_term):
        side_copy(k).start()
    for k in range(1, n_term):
        side_copy(k).wait_recv()
        squares = squares + side_recv[k, scale_rows:]
    inverse = lax.rsqrt(squares + epsilon)
    inverse_ref[...] = inverse
    left_scale = []
    for b in range(blocks):
        picked = jnp.where(part_diagonal, inverse[b : b + 1], 0.0)
        left_scale.append(jnp.sum(picked, axis=1, keepdims=True))

    def finish(m, carry):
        for k in range(1, n_term):
            term_copy(m, k).wait_recv()
        right_scale = inverse_ref[pl.ds(blocks + m, 1)]
        for b in range(blocks):
            total = partial_sum[m, me_term, b]
            for k in range(1, n_term):
                scale = side_recv[k, pl.ds(m * blocks + b, 1)]
                total = total + term_recv[m, k, b].astype(jnp.float32) * scale
            value = total * left_scale[b] * right_scale
            final[m, b] = value
            out_ref[m * blocks + b] = value
        for k in range(1, n_pair):
            pair_copy(m, k).start()
        return carry

    lax.fori_loop(0, n_right, finish, 0)

    def collect(m, carry):
        for k in range(1, n_pair):
            pair_copy(m, k).wait_recv()
            out_ref[pl.ds((k * n_right + m) * blocks, blocks)] = pair_recv[k, m]
        for k in range(1, n_term):
            term_copy(m, k).wait_send()
        for k in range(1, n_pair):
            pair_copy(m, k).wait_send()
        return carry

    lax.fori_loop(0, n_right, collect, 0)
    number_copy.wait()
    for k in range(1, n_term):
        side_copy(k).wait_send()
    for k in range(1, n_doc):
        small_copy(k).wait_send()
        if relay and k == 3:
            relay_copy().wait_send()
        else:
            count_copy(k).wait_send()


def place_kernel(tile_ref, tiles_ref, out_ref, sem):
    def step(row, carry):
        tile = tile_ref[0, row]
        pltpu.make_async_copy(tiles_ref.at[tile], out_ref.at[row], sem).start()
        return carry

    lax.fori_loop(0, out_ref.shape[0], step, 0, unroll=8)
    pltpu.make_async_copy(out_ref, out_ref, sem).wait()


def shards(sizes, counts, block_ids, live_slots, lengths, pairs, pair_count):
    n_doc, n_term, n_pair = sizes
    blocks, slots, rows, cols = counts.shape
    per_core = blocks // n_pair
    n_right = n_doc * per_core
    part_rows = rows // n_term
    table_rows = -(-max(2 * slots, blocks) // 8) * 8
    square_rows = -(-(blocks + n_right) // 8) * 8
    dma = pltpu.SemaphoreType.DMA
    scale_rows = -(-(blocks * n_right) // 8) * 8
    hbm = pl.BlockSpec(memory_space=pltpu.HBM)
    smem = pl.BlockSpec(memory_space=pltpu.SMEM)
    vmem = pl.BlockSpec(memory_space=pltpu.VMEM)
    tiles, numbers = pl.pallas_call(
        functools.partial(tiles_kernel, sizes),
        out_shape=(
            pltpu.VMEM((n_pair * n_right * blocks + 1, part_rows, rows), jnp.float32),
            pltpu.SMEM((1, pairs.shape[0]), jnp.int32),
        ),
        in_specs=[hbm] * 5 + [smem],
        out_specs=(vmem, smem),
        scratch_shapes=[
            pltpu.VMEM((blocks, slots), jnp.int32),
            pltpu.VMEM((blocks, slots), jnp.int32),
            pltpu.VMEM((blocks, slots, rows, cols), jnp.int32),
            pltpu.VMEM((blocks, rows), jnp.int32),
            pltpu.VMEM((2, pairs.shape[0]), jnp.int32),
            pltpu.VMEM((1, pairs.shape[0]), jnp.int32),
            pltpu.VMEM((blocks, slots, rows, cols), jnp.bfloat16),
            pltpu.VMEM((n_doc, blocks + 1, table_rows, cols), jnp.float32),
            pltpu.VMEM((n_doc, per_core, slots, rows, cols), jnp.bfloat16),
            pltpu.VMEM((blocks, slots, rows, cols), jnp.bfloat16),
            pltpu.VMEM((slots, rows, cols), jnp.bfloat16),
            pltpu.VMEM((blocks * rows, slots * cols), jnp.bfloat16),
            pltpu.VMEM(((blocks + n_right) * slots, cols), jnp.float32),
            pltpu.VMEM(((blocks + n_right) * slots, cols), jnp.float32),
            pltpu.VMEM((blocks + n_right, rows, rows), jnp.float32),
            pltpu.VMEM((n_right, n_term, blocks, part_rows, rows), jnp.float32),
            pltpu.VMEM((n_right, n_term, blocks, part_rows, rows), jnp.int16),
            pltpu.VMEM((n_right, n_term, blocks, part_rows, rows), jnp.int16),
            pltpu.VMEM((n_term, scale_rows + square_rows, rows), jnp.float32),
            pltpu.VMEM((n_term, scale_rows + square_rows, rows), jnp.float32),
            pltpu.VMEM((square_rows, rows), jnp.float32),
            pltpu.VMEM((square_rows, rows), jnp.float32),
            pltpu.VMEM((n_right, blocks, part_rows, rows), jnp.float32),
            pltpu.VMEM((n_pair, n_right, blocks, part_rows, rows), jnp.float32),
            dma((5 + blocks,)),
            dma((n_doc,)),
            dma((n_doc,)),
            dma((n_doc,)),
            dma((n_doc,)),
            dma((n_right, n_term)),
            dma((n_right, n_term)),
            dma((n_term,)),
            dma((n_term,)),
            dma((n_right, n_pair)),
            dma((n_right, n_pair)),
        ],
        compiler_params=pltpu.CompilerParams(
            collective_id=0, has_side_effects=True, vmem_limit_bytes=48 * 1024 * 1024
        ),
    )(*[pltpu.with_memory_space_constraint(x, pltpu.HBM) for x in (live_slots, block_ids, counts, lengths.reshape(blocks, rows), pairs.T)], pair_count)
    return pl.pallas_call(
        place_kernel,
        out_shape=jax.ShapeDtypeStruct((pairs.shape[0], part_rows, rows), jnp.float32),
        in_specs=[smem, pl.BlockSpec(memory_space=pl.ANY)],
        out_specs=hbm,
        scratch_shapes=[dma(())],
        compiler_params=pltpu.CompilerParams(vmem_limit_bytes=48 * 1024 * 1024),
    )(numbers, tiles)


def solution(mesh):
    sizes = (mesh.shape["doc"], mesh.shape["term"], mesh.shape["pair"])
    in_specs = (
        P("doc", "term", None, None),
        P("doc", "term"),
        P("doc", "term"),
        P("doc"),
        P(("doc", "pair"), None),
        P(("doc", "pair")),
    )
    out_specs = P(("doc", "pair"), "term", None)
    return jax.shard_map(
        functools.partial(shards, sizes),
        mesh=mesh,
        in_specs=in_specs,
        out_specs=out_specs,
        check_vma=False,
    )
```

```python
import functools

import jax
import jax.numpy as jnp
from jax import lax
from jax.experimental import pallas as pl
from jax.experimental.pallas import tpu as pltpu
from jax.sharding import PartitionSpec as P

steps = 32767.0
tiny = 1e-30
saturation = 1.2
length_weight = 0.75
epsilon = 1e-06

MESH = pl.DeviceIdType.MESH


def exclusive_or(a, b, count):
    result, bit = 0, 1
    while bit < count:
        x, y = lax.rem(a // bit, 2), lax.rem(b // bit, 2)
        result = result + bit * (x + y - 2 * x * y)
        bit *= 2
    return result


def target_of(me, k, count):
    if count & (count - 1):
        return lax.rem(me + k, count)
    return exclusive_or(me, k, count)


def slot_of(me, owner, count):
    if count & (count - 1):
        return lax.rem(me - owner + count, count)
    return exclusive_or(me, owner, count)


def tiles_kernel(
    sizes,
    live_hbm,
    ids_hbm,
    counts_hbm,
    lengths_hbm,
    pairs_hbm,
    limit_ref,
    out_ref,
    tile_ref,
    live_ref,
    ids_ref,
    counts_ref,
    lengths_ref,
    pairs_ref,
    number_ref,
    masked,
    small,
    right_counts,
    left_weight,
    right_weight,
    aligned,
    ids_table,
    freq_table,
    length_table,
    partial_sum,
    coded,
    term_recv,
    side_own,
    side_recv,
    square_own,
    inverse_ref,
    final,
    pair_recv,
    load_sem,
    small_send_sem,
    small_recv_sem,
    count_send_sem,
    count_recv_sem,
    term_send_sem,
    term_recv_sem,
    side_send_sem,
    side_recv_sem,
    pair_send_sem,
    pair_recv_sem,
):
    n_doc, n_term, n_pair = sizes
    blocks, slots, rows, cols = counts_ref.shape
    per_core = blocks // n_pair
    n_right = n_doc * per_core
    part_rows = rows // n_term
    docs_all = n_doc * blocks * rows
    me_doc = lax.axis_index("doc")
    me_term = lax.axis_index("term")
    me_pair = lax.axis_index("pair")

    def doc_peer(k):
        return {"doc": target_of(me_doc, k, n_doc)}

    def term_peer(k):
        return {"term": lax.rem(me_term + k, n_term)}

    def pair_peer(k):
        return {"pair": lax.rem(me_pair + k, n_pair)}

    def small_copy(k):
        return pltpu.make_async_remote_copy(
            src_ref=small.at[0],
            dst_ref=small.at[k],
            send_sem=small_send_sem.at[k],
            recv_sem=small_recv_sem.at[k],
            device_id=doc_peer(k),
            device_id_type=MESH,
        )

    def count_copy(k):
        return pltpu.make_async_remote_copy(
            src_ref=masked.at[pl.ds(me_pair * per_core, per_core)],
            dst_ref=right_counts.at[k],
            send_sem=count_send_sem.at[k],
            recv_sem=count_recv_sem.at[k],
            device_id=doc_peer(k),
            device_id_type=MESH,
        )

    relay = False
    near = 1 + lax.rem(me_pair, 2)
    far = 3 - near

    def relay_copy():
        return pltpu.make_async_remote_copy(
            src_ref=right_counts.at[near],
            dst_ref=right_counts.at[3],
            send_sem=count_send_sem.at[3],
            recv_sem=count_recv_sem.at[3],
            device_id=doc_peer(far),
            device_id_type=MESH,
        )

    def term_copy(m, k):
        return pltpu.make_async_remote_copy(
            src_ref=coded.at[m, lax.rem(me_term + k, n_term)],
            dst_ref=term_recv.at[m, k],
            send_sem=term_send_sem.at[m, k],
            recv_sem=term_recv_sem.at[m, k],
            device_id=term_peer(k),
            device_id_type=MESH,
        )

    def side_copy(k):
        return pltpu.make_async_remote_copy(
            src_ref=side_own.at[lax.rem(me_term + k, n_term)],
            dst_ref=side_recv.at[k],
            send_sem=side_send_sem.at[k],
            recv_sem=side_recv_sem.at[k],
            device_id=term_peer(k),
            device_id_type=MESH,
        )

    def pair_copy(m, k):
        return pltpu.make_async_remote_copy(
            src_ref=final.at[m],
            dst_ref=pair_recv.at[k, m],
            send_sem=pair_send_sem.at[m, k],
            recv_sem=pair_recv_sem.at[m, k],
            device_id=pair_peer(k),
            device_id_type=MESH,
        )

    barrier = pltpu.get_barrier_semaphore()
    for k in range(1, n_doc):
        pl.semaphore_signal(barrier, inc=1, device_id=doc_peer(k), device_id_type=MESH)
    for k in range(1, n_term):
        pl.semaphore_signal(barrier, inc=1, device_id=term_peer(k), device_id_type=MESH)
    for k in range(1, n_pair):
        pl.semaphore_signal(barrier, inc=1, device_id=pair_peer(k), device_id_type=MESH)

    loads = [
        pltpu.make_async_copy(live_hbm, live_ref, load_sem.at[0]),
        pltpu.make_async_copy(ids_hbm, ids_ref, load_sem.at[1]),
        pltpu.make_async_copy(lengths_hbm, lengths_ref, load_sem.at[2]),
    ]
    extra = [pltpu.make_async_copy(pairs_hbm, pairs_ref, load_sem.at[3 + blocks])]
    loads += [
        pltpu.make_async_copy(counts_hbm.at[b], counts_ref.at[b], load_sem.at[3 + b])
        for b in range(blocks)
    ]
    for load in loads + extra:
        load.start()
    small[0] = jnp.zeros(small.shape[1:], jnp.float32)
    square_own[...] = jnp.zeros(square_own.shape, jnp.float32)
    out_ref[out_ref.shape[0] - 1] = jnp.zeros(out_ref.shape[1:], jnp.float32)
    for load in loads[:3]:
        load.wait()
    for b in range(blocks):
        loads[3 + b].wait()
        for s in range(slots):
            live = jnp.broadcast_to(live_ref[b : b + 1, s : s + 1], (rows, cols)) > 0
            value = jnp.where(live, counts_ref[b, s].astype(jnp.float32), 0.0)
            masked[b, s] = value.astype(jnp.bfloat16)
            small[0, b, s : s + 1] = jnp.sum(
                jnp.where(value > 0.0, 1.0, 0.0), axis=0, keepdims=True
            )
            small[0, b, slots + s : slots + s + 1] = jnp.broadcast_to(
                ids_ref[b : b + 1, s : s + 1], (1, cols)
            ).astype(jnp.float32)
    small[0, blocks, 0:blocks] = lengths_ref[...].astype(jnp.float32)

    pl.semaphore_wait(barrier, n_doc + n_term + n_pair - 3)

    for k in range(1, n_doc):
        small_copy(k).start()
    for k in (near, far) if relay else range(1, n_doc):
        count_copy(k).start()
    for k in range(1, n_doc):
        small_copy(k).wait_recv()

    row_at = lax.broadcasted_iota(jnp.int32, (rows, cols), 0)
    col_at = lax.broadcasted_iota(jnp.int32, (rows, cols), 1)
    diagonal = row_at == col_at
    part_diagonal = row_at[:part_rows] + me_term * part_rows == col_at[:part_rows]
    total_len = lax.fori_loop(
        0,
        n_doc,
        lambda k, acc: acc + jnp.sum(small[k, blocks], axis=0, keepdims=True),
        jnp.zeros((1, cols), jnp.float32),
    )
    avg_len = jnp.sum(total_len, axis=1, keepdims=True) / docs_all

    def table_row(k, b, place):
        ids_table[pl.ds(place * slots, slots)] = small[k, b, slots : 2 * slots]
        length = small[k, blocks, pl.ds(b, 1)]
        scale = saturation * (1.0 - length_weight + length_weight * length / avg_len)
        scale = jnp.sum(jnp.where(diagonal, scale, 0.0), axis=1, keepdims=True)
        length_table[place] = jnp.broadcast_to(scale, (rows, cols))

    for b in range(blocks):
        table_row(0, b, b)

    def right_rows(k, carry):
        for i in range(per_core):
            table_row(k, me_pair * per_core + i, blocks + k * per_core + i)
        return carry

    lax.fori_loop(0, n_doc, right_rows, 0, unroll=min(n_doc, 4))
    ids = ids_table[...]

    def add(k, acc):
        for b in range(blocks):
            table = small[k, b]
            for s in range(slots):
                same = ids == table[slots + s : slots + s + 1]
                acc = acc + jnp.where(same, table[s : s + 1], 0.0)
        return acc

    doc_freq = lax.fori_loop(
        0, n_doc, add, jnp.zeros(ids.shape, jnp.float32), unroll=min(n_doc, 4)
    )
    freq_table[...] = jnp.log(1.0 + (docs_all - doc_freq + 0.5) / (doc_freq + 0.5)) * (
        saturation + 1.0
    )

    def weigh(read, target, place):
        squares = jnp.zeros((rows, cols), jnp.float32)
        for s in range(slots):
            freq = read(s).astype(jnp.float32)
            weight = freq_table[pl.ds(place * slots + s, 1)] * freq / (freq + length_table[place])
            squares = squares + weight * weight
            target[s] = weight.astype(jnp.bfloat16)
        return squares

    def keep_squares(squares, place):
        squares = jnp.sum(squares, axis=1, keepdims=True)
        squares = jnp.where(diagonal, squares, 0.0)
        square_own[pl.ds(place, 1)] = jnp.sum(squares, axis=0, keepdims=True)

    def align(m, right_ids):
        for b in range(blocks):
            left_ids = small[0, b, slots : 2 * slots]
            for j in range(slots):
                total = jnp.zeros((rows, cols), jnp.bfloat16)
                for i in range(slots):
                    same = left_ids[i : i + 1] == right_ids[j : j + 1]
                    same = jnp.where(same, 1.0, 0.0).astype(jnp.bfloat16)
                    total = total + left_weight[b, i] * same
                aligned[m, b * rows : (b + 1) * rows, j * cols : (j + 1) * cols] = total

    def grams(m, right):
        gram = lax.dot_general(
            aligned[m],
            jnp.concatenate([right[j] for j in range(slots)], axis=1),
            (((1,), (1,)), ((), ())),
            preferred_element_type=jnp.float32,
        )
        for z in range(n_term):
            for b in range(blocks):
                start = b * rows + z * part_rows
                piece = gram[start : start + part_rows]
                top = jnp.maximum(jnp.max(piece, axis=0, keepdims=True), tiny)
                partial_sum[m, z, b] = piece
                code = (piece * (steps / top) + 0.5).astype(jnp.int32)
                coded[m, z, b] = code.astype(jnp.int16)
                side_own[z, pl.ds(m * blocks + b, 1)] = top * (1.0 / steps)
        for k in range(1, n_term):
            term_copy(m, k).start()

    left_squares = [
        weigh(lambda s, b=b: masked[b, s], left_weight.at[b], b) for b in range(blocks)
    ]
    for i in range(per_core):
        own = me_pair * per_core + i
        align(i, small[0, own, slots : 2 * slots])
        grams(i, left_weight.at[own])
    if relay:
        count_copy(near).wait_recv()
        relay_copy().start()

    def align_right(k, carry):
        for i in range(per_core):
            align(k * per_core + i, small[k, me_pair * per_core + i, slots : 2 * slots])
        return carry

    lax.fori_loop(1, n_doc, align_right, 0)
    for load in extra:
        load.wait()
    left = pairs_ref[0:1]
    right = pairs_ref[1:2]
    number = left - me_doc * blocks
    for block in range(n_doc * blocks):
        owner, inner = block // blocks, block % blocks
        side = lax.rem(me_pair - inner // per_core + n_pair, n_pair)
        m = slot_of(me_doc, owner, n_doc) * per_core + inner % per_core
        number = number + jnp.where(right == block, (side * n_right + m) * blocks, 0)
    row = lax.broadcasted_iota(jnp.int32, number.shape, 1)
    number_ref[...] = jnp.where(row < limit_ref[0], number, out_ref.shape[0] - 1)
    number_copy = pltpu.make_async_copy(number_ref, tile_ref, load_sem.at[4 + blocks])
    number_copy.start()

    for b in range(blocks):
        keep_squares(left_squares[b], b)
    for i in range(per_core):
        square_own[pl.ds(blocks + i, 1)] = square_own[pl.ds(me_pair * per_core + i, 1)]

    def right_step(step, carry):
        if relay:
            k = jnp.where(step == 1, near, jnp.where(step == 2, far, 3))

            @pl.when(step == 2)
            def _():
                count_copy(far).wait_recv()

            @pl.when(step == 3)
            def _():
                relay_copy().wait_recv()
        else:
            k = step
            count_copy(k).wait_recv()
        for i in range(per_core):
            m = k * per_core + i
            squares = weigh(lambda s, i=i: right_counts[k, i, s], right_weight, blocks + m)
            grams(m, right_weight)
            keep_squares(squares, blocks + m)
        return carry

    lax.fori_loop(1, n_doc, right_step, 0)

    scale_rows = side_own.shape[1] - square_own.shape[0]
    squares = square_own[...]
    for z in range(n_term):
        side_own[z, scale_rows:] = squares
    for k in range(1, n_term):
        side_copy(k).start()
    for k in range(1, n_term):
        side_copy(k).wait_recv()
        squares = squares + side_recv[k, scale_rows:]
    inverse = lax.rsqrt(squares + epsilon)
    inverse_ref[...] = inverse
    left_scale = []
    for b in range(blocks):
        picked = jnp.where(part_diagonal, inverse[b : b + 1], 0.0)
        left_scale.append(jnp.sum(picked, axis=1, keepdims=True))

    def finish(m, carry):
        for k in range(1, n_term):
            term_copy(m, k).wait_recv()
        right_scale = inverse_ref[pl.ds(blocks + m, 1)]
        for b in range(blocks):
            total = partial_sum[m, me_term, b]
            for k in range(1, n_term):
                scale = side_recv[k, pl.ds(m * blocks + b, 1)]
                total = total + term_recv[m, k, b].astype(jnp.float32) * scale
            value = total * left_scale[b] * right_scale
            final[m, b] = value
            out_ref[m * blocks + b] = value
        for k in range(1, n_pair):
            pair_copy(m, k).start()
        return carry

    lax.fori_loop(0, n_right, finish, 0)

    def collect(m, carry):
        for k in range(1, n_pair):
            pair_copy(m, k).wait_recv()
            out_ref[pl.ds((k * n_right + m) * blocks, blocks)] = pair_recv[k, m]
        for k in range(1, n_term):
            term_copy(m, k).wait_send()
        for k in range(1, n_pair):
            pair_copy(m, k).wait_send()
        return carry

    lax.fori_loop(0, n_right, collect, 0)
    number_copy.wait()
    for k in range(1, n_term):
        side_copy(k).wait_send()
    for k in range(1, n_doc):
        small_copy(k).wait_send()
        if relay and k == 3:
            relay_copy().wait_send()
        else:
            count_copy(k).wait_send()


def place_kernel(tile_ref, tiles_ref, out_ref, sem):
    def step(row, carry):
        tile = tile_ref[0, row]
        pltpu.make_async_copy(tiles_ref.at[tile], out_ref.at[row], sem).start()
        return carry

    lax.fori_loop(0, out_ref.shape[0], step, 0, unroll=8)
    pltpu.make_async_copy(out_ref, out_ref, sem).wait()


def shards(sizes, counts, block_ids, live_slots, lengths, pairs, pair_count):
    n_doc, n_term, n_pair = sizes
    blocks, slots, rows, cols = counts.shape
    per_core = blocks // n_pair
    n_right = n_doc * per_core
    part_rows = rows // n_term
    table_rows = -(-max(2 * slots, blocks) // 8) * 8
    square_rows = -(-(blocks + n_right) // 8) * 8
    dma = pltpu.SemaphoreType.DMA
    scale_rows = -(-(blocks * n_right) // 8) * 8
    hbm = pl.BlockSpec(memory_space=pltpu.HBM)
    smem = pl.BlockSpec(memory_space=pltpu.SMEM)
    vmem = pl.BlockSpec(memory_space=pltpu.VMEM)
    tiles, numbers = pl.pallas_call(
        functools.partial(tiles_kernel, sizes),
        out_shape=(
            pltpu.VMEM((n_pair * n_right * blocks + 1, part_rows, rows), jnp.float32),
            pltpu.SMEM((1, pairs.shape[0]), jnp.int32),
        ),
        in_specs=[hbm] * 5 + [smem],
        out_specs=(vmem, smem),
        scratch_shapes=[
            pltpu.VMEM((blocks, slots), jnp.int32),
            pltpu.VMEM((blocks, slots), jnp.int32),
            pltpu.VMEM((blocks, slots, rows, cols), jnp.int32),
            pltpu.VMEM((blocks, rows), jnp.int32),
            pltpu.VMEM((2, pairs.shape[0]), jnp.int32),
            pltpu.VMEM((1, pairs.shape[0]), jnp.int32),
            pltpu.VMEM((blocks, slots, rows, cols), jnp.bfloat16),
            pltpu.VMEM((n_doc, blocks + 1, table_rows, cols), jnp.float32),
            pltpu.VMEM((n_doc, per_core, slots, rows, cols), jnp.bfloat16),
            pltpu.VMEM((blocks, slots, rows, cols), jnp.bfloat16),
            pltpu.VMEM((slots, rows, cols), jnp.bfloat16),
            pltpu.VMEM((n_right, blocks * rows, slots * cols), jnp.bfloat16),
            pltpu.VMEM(((blocks + n_right) * slots, cols), jnp.float32),
            pltpu.VMEM(((blocks + n_right) * slots, cols), jnp.float32),
            pltpu.VMEM((blocks + n_right, rows, rows), jnp.float32),
            pltpu.VMEM((n_right, n_term, blocks, part_rows, rows), jnp.float32),
            pltpu.VMEM((n_right, n_term, blocks, part_rows, rows), jnp.int16),
            pltpu.VMEM((n_right, n_term, blocks, part_rows, rows), jnp.int16),
            pltpu.VMEM((n_term, scale_rows + square_rows, rows), jnp.float32),
            pltpu.VMEM((n_term, scale_rows + square_rows, rows), jnp.float32),
            pltpu.VMEM((square_rows, rows), jnp.float32),
            pltpu.VMEM((square_rows, rows), jnp.float32),
            pltpu.VMEM((n_right, blocks, part_rows, rows), jnp.float32),
            pltpu.VMEM((n_pair, n_right, blocks, part_rows, rows), jnp.float32),
            dma((5 + blocks,)),
            dma((n_doc,)),
            dma((n_doc,)),
            dma((n_doc,)),
            dma((n_doc,)),
            dma((n_right, n_term)),
            dma((n_right, n_term)),
            dma((n_term,)),
            dma((n_term,)),
            dma((n_right, n_pair)),
            dma((n_right, n_pair)),
        ],
        compiler_params=pltpu.CompilerParams(
            collective_id=0, has_side_effects=True, vmem_limit_bytes=48 * 1024 * 1024
        ),
    )(*[pltpu.with_memory_space_constraint(x, pltpu.HBM) for x in (live_slots, block_ids, counts, lengths.reshape(blocks, rows), pairs.T)], pair_count)
    return pl.pallas_call(
        place_kernel,
        out_shape=jax.ShapeDtypeStruct((pairs.shape[0], part_rows, rows), jnp.float32),
        in_specs=[smem, pl.BlockSpec(memory_space=pl.ANY)],
        out_specs=hbm,
        scratch_shapes=[dma(())],
        compiler_params=pltpu.CompilerParams(vmem_limit_bytes=48 * 1024 * 1024),
    )(numbers, tiles)


def solution(mesh):
    sizes = (mesh.shape["doc"], mesh.shape["term"], mesh.shape["pair"])
    in_specs = (
        P("doc", "term", None, None),
        P("doc", "term"),
        P("doc", "term"),
        P("doc"),
        P(("doc", "pair"), None),
        P(("doc", "pair")),
    )
    out_specs = P(("doc", "pair"), "term", None)
    return jax.shard_map(
        functools.partial(shards, sizes),
        mesh=mesh,
        in_specs=in_specs,
        out_specs=out_specs,
        check_vma=False,
    )
```

```python
import functools

import jax
import jax.numpy as jnp
from jax import lax
from jax.experimental import pallas as pl
from jax.experimental.pallas import tpu as pltpu
from jax.sharding import PartitionSpec as P

steps = 32767.0
tiny = 1e-30
saturation = 1.2
length_weight = 0.75
epsilon = 1e-06

MESH = pl.DeviceIdType.MESH


def exclusive_or(a, b, count):
    result, bit = 0, 1
    while bit < count:
        x, y = lax.rem(a // bit, 2), lax.rem(b // bit, 2)
        result = result + bit * (x + y - 2 * x * y)
        bit *= 2
    return result


def target_of(me, k, count):
    if count & (count - 1):
        return lax.rem(me + k, count)
    return exclusive_or(me, k, count)


def slot_of(me, owner, count):
    if count & (count - 1):
        return lax.rem(me - owner + count, count)
    return exclusive_or(me, owner, count)


def tiles_kernel(
    sizes,
    live_hbm,
    ids_hbm,
    counts_hbm,
    lengths_hbm,
    pairs_hbm,
    limit_ref,
    out_ref,
    tile_ref,
    live_ref,
    ids_ref,
    counts_ref,
    lengths_ref,
    pairs_ref,
    number_ref,
    masked,
    small,
    right_counts,
    left_weight,
    right_weight,
    aligned,
    ids_table,
    freq_table,
    length_table,
    partial_sum,
    coded,
    term_recv,
    side_own,
    side_recv,
    square_own,
    inverse_ref,
    final,
    pair_recv,
    load_sem,
    small_send_sem,
    small_recv_sem,
    count_send_sem,
    count_recv_sem,
    term_send_sem,
    term_recv_sem,
    side_send_sem,
    side_recv_sem,
    pair_send_sem,
    pair_recv_sem,
):
    n_doc, n_term, n_pair = sizes
    blocks, slots, rows, cols = counts_ref.shape
    per_core = blocks // n_pair
    n_right = n_doc * per_core
    part_rows = rows // n_term
    docs_all = n_doc * blocks * rows
    me_doc = lax.axis_index("doc")
    me_term = lax.axis_index("term")
    me_pair = lax.axis_index("pair")

    def doc_peer(k):
        return {"doc": target_of(me_doc, k, n_doc)}

    def term_peer(k):
        return {"term": lax.rem(me_term + k, n_term)}

    def pair_peer(k):
        return {"pair": lax.rem(me_pair + k, n_pair)}

    def small_copy(k):
        return pltpu.make_async_remote_copy(
            src_ref=small.at[0],
            dst_ref=small.at[k],
            send_sem=small_send_sem.at[k],
            recv_sem=small_recv_sem.at[k],
            device_id=doc_peer(k),
            device_id_type=MESH,
        )

    def count_copy(k):
        return pltpu.make_async_remote_copy(
            src_ref=masked.at[pl.ds(me_pair * per_core, per_core)],
            dst_ref=right_counts.at[k],
            send_sem=count_send_sem.at[k],
            recv_sem=count_recv_sem.at[k],
            device_id=doc_peer(k),
            device_id_type=MESH,
        )

    def term_copy(m, k):
        return pltpu.make_async_remote_copy(
            src_ref=coded.at[m, lax.rem(me_term + k, n_term)],
            dst_ref=term_recv.at[m, k],
            send_sem=term_send_sem.at[m, k],
            recv_sem=term_recv_sem.at[m, k],
            device_id=term_peer(k),
            device_id_type=MESH,
        )

    def side_copy(k):
        return pltpu.make_async_remote_copy(
            src_ref=side_own.at[lax.rem(me_term + k, n_term)],
            dst_ref=side_recv.at[k],
            send_sem=side_send_sem.at[k],
            recv_sem=side_recv_sem.at[k],
            device_id=term_peer(k),
            device_id_type=MESH,
        )

    def pair_copy(m, k):
        return pltpu.make_async_remote_copy(
            src_ref=final.at[m],
            dst_ref=pair_recv.at[k, m],
            send_sem=pair_send_sem.at[m, k],
            recv_sem=pair_recv_sem.at[m, k],
            device_id=pair_peer(k),
            device_id_type=MESH,
        )

    barrier = pltpu.get_barrier_semaphore()
    for k in range(1, n_doc):
        pl.semaphore_signal(barrier, inc=1, device_id=doc_peer(k), device_id_type=MESH)
    for k in range(1, n_term):
        pl.semaphore_signal(barrier, inc=1, device_id=term_peer(k), device_id_type=MESH)
    for k in range(1, n_pair):
        pl.semaphore_signal(barrier, inc=1, device_id=pair_peer(k), device_id_type=MESH)

    loads = [
        pltpu.make_async_copy(live_hbm, live_ref, load_sem.at[0]),
        pltpu.make_async_copy(ids_hbm, ids_ref, load_sem.at[1]),
        pltpu.make_async_copy(lengths_hbm, lengths_ref, load_sem.at[2]),
    ]
    extra = [pltpu.make_async_copy(pairs_hbm, pairs_ref, load_sem.at[3 + blocks])]
    loads += [
        pltpu.make_async_copy(counts_hbm.at[b], counts_ref.at[b], load_sem.at[3 + b])
        for b in range(blocks)
    ]
    for load in loads + extra:
        load.start()
    small[0] = jnp.zeros(small.shape[1:], jnp.float32)
    square_own[...] = jnp.zeros(square_own.shape, jnp.float32)
    out_ref[out_ref.shape[0] - 1] = jnp.zeros(out_ref.shape[1:], jnp.float32)
    for load in loads[:3]:
        load.wait()
    for b in range(blocks):
        loads[3 + b].wait()
        for s in range(slots):
            live = jnp.broadcast_to(live_ref[b : b + 1, s : s + 1], (rows, cols)) > 0
            value = jnp.where(live, counts_ref[b, s].astype(jnp.float32), 0.0)
            masked[b, s] = value.astype(jnp.bfloat16)
            small[0, b, s : s + 1] = jnp.sum(
                jnp.where(value > 0.0, 1.0, 0.0), axis=0, keepdims=True
            )
            small[0, b, slots + s : slots + s + 1] = jnp.broadcast_to(
                ids_ref[b : b + 1, s : s + 1], (1, cols)
            ).astype(jnp.float32)
    small[0, blocks, 0:blocks] = lengths_ref[...].astype(jnp.float32)

    pl.semaphore_wait(barrier, n_doc + n_term + n_pair - 3)

    for k in range(1, n_doc):
        small_copy(k).start()
    first = [k for k in range(1, n_doc) if k & (k - 1) == 0]
    for k in first:
        count_copy(k).start()
    for k in range(1, n_doc):
        small_copy(k).wait_recv()

    row_at = lax.broadcasted_iota(jnp.int32, (rows, cols), 0)
    col_at = lax.broadcasted_iota(jnp.int32, (rows, cols), 1)
    diagonal = row_at == col_at
    part_diagonal = row_at[:part_rows] + me_term * part_rows == col_at[:part_rows]
    total_len = lax.fori_loop(
        0,
        n_doc,
        lambda k, acc: acc + jnp.sum(small[k, blocks], axis=0, keepdims=True),
        jnp.zeros((1, cols), jnp.float32),
    )
    avg_len = jnp.sum(total_len, axis=1, keepdims=True) / docs_all

    def table_row(k, b, place):
        ids_table[pl.ds(place * slots, slots)] = small[k, b, slots : 2 * slots]
        length = small[k, blocks, pl.ds(b, 1)]
        scale = saturation * (1.0 - length_weight + length_weight * length / avg_len)
        scale = jnp.sum(jnp.where(diagonal, scale, 0.0), axis=1, keepdims=True)
        length_table[place] = jnp.broadcast_to(scale, (rows, cols))

    for b in range(blocks):
        table_row(0, b, b)

    def right_rows(k, carry):
        for i in range(per_core):
            table_row(k, me_pair * per_core + i, blocks + k * per_core + i)
        return carry

    lax.fori_loop(0, n_doc, right_rows, 0, unroll=min(n_doc, 4))
    ids = ids_table[...]

    def add(k, acc):
        for b in range(blocks):
            table = small[k, b]
            for s in range(slots):
                same = ids == table[slots + s : slots + s + 1]
                acc = acc + jnp.where(same, table[s : s + 1], 0.0)
        return acc

    doc_freq = lax.fori_loop(
        0, n_doc, add, jnp.zeros(ids.shape, jnp.float32), unroll=min(n_doc, 4)
    )
    freq_table[...] = jnp.log(1.0 + (docs_all - doc_freq + 0.5) / (doc_freq + 0.5)) * (
        saturation + 1.0
    )

    def weigh(read, target, place):
        squares = jnp.zeros((rows, cols), jnp.float32)
        for s in range(slots):
            freq = read(s).astype(jnp.float32)
            weight = freq_table[pl.ds(place * slots + s, 1)] * freq / (freq + length_table[place])
            squares = squares + weight * weight
            target[s] = weight.astype(jnp.bfloat16)
        return squares

    def keep_squares(squares, place):
        squares = jnp.sum(squares, axis=1, keepdims=True)
        squares = jnp.where(diagonal, squares, 0.0)
        square_own[pl.ds(place, 1)] = jnp.sum(squares, axis=0, keepdims=True)

    def align(m, right_ids):
        for b in range(blocks):
            left_ids = small[0, b, slots : 2 * slots]
            for j in range(slots):
                total = jnp.zeros((rows, cols), jnp.bfloat16)
                for i in range(slots):
                    same = left_ids[i : i + 1] == right_ids[j : j + 1]
                    same = jnp.where(same, 1.0, 0.0).astype(jnp.bfloat16)
                    total = total + left_weight[b, i] * same
                aligned[m, b * rows : (b + 1) * rows, j * cols : (j + 1) * cols] = total

    def grams(m, right):
        gram = lax.dot_general(
            aligned[m],
            jnp.concatenate([right[j] for j in range(slots)], axis=1),
            (((1,), (1,)), ((), ())),
            preferred_element_type=jnp.float32,
        )
        for z in range(n_term):
            for b in range(blocks):
                start = b * rows + z * part_rows
                piece = gram[start : start + part_rows]
                top = jnp.maximum(jnp.max(piece, axis=0, keepdims=True), tiny)
                partial_sum[m, z, b] = piece
                code = (piece * (steps / top) + 0.5).astype(jnp.int32)
                coded[m, z, b] = code.astype(jnp.int16)
                side_own[z, pl.ds(m * blocks + b, 1)] = top * (1.0 / steps)
        for k in range(1, n_term):
            term_copy(m, k).start()

    left_squares = [
        weigh(lambda s, b=b: masked[b, s], left_weight.at[b], b) for b in range(blocks)
    ]
    for k in range(1, n_doc):
        if k not in first:
            count_copy(k).start()
    for i in range(per_core):
        own = me_pair * per_core + i
        align(i, small[0, own, slots : 2 * slots])
        grams(i, left_weight.at[own])

    def align_right(k, carry):
        for i in range(per_core):
            align(k * per_core + i, small[k, me_pair * per_core + i, slots : 2 * slots])
        return carry

    lax.fori_loop(1, n_doc, align_right, 0)
    for load in extra:
        load.wait()
    left = pairs_ref[0:1]
    right = pairs_ref[1:2]
    number = left - me_doc * blocks
    for block in range(n_doc * blocks):
        owner, inner = block // blocks, block % blocks
        side = lax.rem(me_pair - inner // per_core + n_pair, n_pair)
        m = slot_of(me_doc, owner, n_doc) * per_core + inner % per_core
        number = number + jnp.where(right == block, (side * n_right + m) * blocks, 0)
    row = lax.broadcasted_iota(jnp.int32, number.shape, 1)
    number_ref[...] = jnp.where(row < limit_ref[0], number, out_ref.shape[0] - 1)
    number_copy = pltpu.make_async_copy(number_ref, tile_ref, load_sem.at[4 + blocks])
    number_copy.start()

    for b in range(blocks):
        keep_squares(left_squares[b], b)
    for i in range(per_core):
        square_own[pl.ds(blocks + i, 1)] = square_own[pl.ds(me_pair * per_core + i, 1)]

    def right_step(k, carry):
        count_copy(k).wait_recv()
        for i in range(per_core):
            m = k * per_core + i
            squares = weigh(lambda s, i=i: right_counts[k, i, s], right_weight, blocks + m)
            grams(m, right_weight)
            keep_squares(squares, blocks + m)
        return carry

    lax.fori_loop(1, n_doc, right_step, 0)

    scale_rows = side_own.shape[1] - square_own.shape[0]
    squares = square_own[...]
    for z in range(n_term):
        side_own[z, scale_rows:] = squares
    for k in range(1, n_term):
        side_copy(k).start()
    for k in range(1, n_term):
        side_copy(k).wait_recv()
        squares = squares + side_recv[k, scale_rows:]
    inverse = lax.rsqrt(squares + epsilon)
    inverse_ref[...] = inverse
    left_scale = []
    for b in range(blocks):
        picked = jnp.where(part_diagonal, inverse[b : b + 1], 0.0)
        left_scale.append(jnp.sum(picked, axis=1, keepdims=True))

    def finish(m, carry):
        for k in range(1, n_term):
            term_copy(m, k).wait_recv()
        right_scale = inverse_ref[pl.ds(blocks + m, 1)]
        for b in range(blocks):
            total = partial_sum[m, me_term, b]
            for k in range(1, n_term):
                scale = side_recv[k, pl.ds(m * blocks + b, 1)]
                total = total + term_recv[m, k, b].astype(jnp.float32) * scale
            value = total * left_scale[b] * right_scale
            final[m, b] = value
            out_ref[m * blocks + b] = value
        for k in range(1, n_pair):
            pair_copy(m, k).start()
        return carry

    lax.fori_loop(0, n_right, finish, 0)

    def collect(m, carry):
        for k in range(1, n_pair):
            pair_copy(m, k).wait_recv()
            out_ref[pl.ds((k * n_right + m) * blocks, blocks)] = pair_recv[k, m]
        for k in range(1, n_term):
            term_copy(m, k).wait_send()
        for k in range(1, n_pair):
            pair_copy(m, k).wait_send()
        return carry

    lax.fori_loop(0, n_right, collect, 0)
    number_copy.wait()
    for k in range(1, n_term):
        side_copy(k).wait_send()
    for k in range(1, n_doc):
        small_copy(k).wait_send()
        count_copy(k).wait_send()


def place_kernel(tile_ref, tiles_ref, out_ref, sem):
    def step(row, carry):
        tile = tile_ref[0, row]
        pltpu.make_async_copy(tiles_ref.at[tile], out_ref.at[row], sem).start()
        return carry

    lax.fori_loop(0, out_ref.shape[0], step, 0, unroll=8)
    pltpu.make_async_copy(out_ref, out_ref, sem).wait()


def shards(sizes, counts, block_ids, live_slots, lengths, pairs, pair_count):
    n_doc, n_term, n_pair = sizes
    blocks, slots, rows, cols = counts.shape
    per_core = blocks // n_pair
    n_right = n_doc * per_core
    part_rows = rows // n_term
    table_rows = -(-max(2 * slots, blocks) // 8) * 8
    square_rows = -(-(blocks + n_right) // 8) * 8
    dma = pltpu.SemaphoreType.DMA
    scale_rows = -(-(blocks * n_right) // 8) * 8
    hbm = pl.BlockSpec(memory_space=pltpu.HBM)
    smem = pl.BlockSpec(memory_space=pltpu.SMEM)
    vmem = pl.BlockSpec(memory_space=pltpu.VMEM)
    tiles, numbers = pl.pallas_call(
        functools.partial(tiles_kernel, sizes),
        out_shape=(
            pltpu.VMEM((n_pair * n_right * blocks + 1, part_rows, rows), jnp.float32),
            pltpu.SMEM((1, pairs.shape[0]), jnp.int32),
        ),
        in_specs=[hbm] * 5 + [smem],
        out_specs=(vmem, smem),
        scratch_shapes=[
            pltpu.VMEM((blocks, slots), jnp.int32),
            pltpu.VMEM((blocks, slots), jnp.int32),
            pltpu.VMEM((blocks, slots, rows, cols), jnp.int32),
            pltpu.VMEM((blocks, rows), jnp.int32),
            pltpu.VMEM((2, pairs.shape[0]), jnp.int32),
            pltpu.VMEM((1, pairs.shape[0]), jnp.int32),
            pltpu.VMEM((blocks, slots, rows, cols), jnp.bfloat16),
            pltpu.VMEM((n_doc, blocks + 1, table_rows, cols), jnp.float32),
            pltpu.VMEM((n_doc, per_core, slots, rows, cols), jnp.bfloat16),
            pltpu.VMEM((blocks, slots, rows, cols), jnp.bfloat16),
            pltpu.VMEM((slots, rows, cols), jnp.bfloat16),
            pltpu.VMEM((n_right, blocks * rows, slots * cols), jnp.bfloat16),
            pltpu.VMEM(((blocks + n_right) * slots, cols), jnp.float32),
            pltpu.VMEM(((blocks + n_right) * slots, cols), jnp.float32),
            pltpu.VMEM((blocks + n_right, rows, rows), jnp.float32),
            pltpu.VMEM((n_right, n_term, blocks, part_rows, rows), jnp.float32),
            pltpu.VMEM((n_right, n_term, blocks, part_rows, rows), jnp.int16),
            pltpu.VMEM((n_right, n_term, blocks, part_rows, rows), jnp.int16),
            pltpu.VMEM((n_term, scale_rows + square_rows, rows), jnp.float32),
            pltpu.VMEM((n_term, scale_rows + square_rows, rows), jnp.float32),
            pltpu.VMEM((square_rows, rows), jnp.float32),
            pltpu.VMEM((square_rows, rows), jnp.float32),
            pltpu.VMEM((n_right, blocks, part_rows, rows), jnp.float32),
            pltpu.VMEM((n_pair, n_right, blocks, part_rows, rows), jnp.float32),
            dma((5 + blocks,)),
            dma((n_doc,)),
            dma((n_doc,)),
            dma((n_doc,)),
            dma((n_doc,)),
            dma((n_right, n_term)),
            dma((n_right, n_term)),
            dma((n_term,)),
            dma((n_term,)),
            dma((n_right, n_pair)),
            dma((n_right, n_pair)),
        ],
        compiler_params=pltpu.CompilerParams(
            collective_id=0, has_side_effects=True, vmem_limit_bytes=48 * 1024 * 1024
        ),
    )(*[pltpu.with_memory_space_constraint(x, pltpu.HBM) for x in (live_slots, block_ids, counts, lengths.reshape(blocks, rows), pairs.T)], pair_count)
    return pl.pallas_call(
        place_kernel,
        out_shape=jax.ShapeDtypeStruct((pairs.shape[0], part_rows, rows), jnp.float32),
        in_specs=[smem, pl.BlockSpec(memory_space=pl.ANY)],
        out_specs=hbm,
        scratch_shapes=[dma(())],
        compiler_params=pltpu.CompilerParams(vmem_limit_bytes=48 * 1024 * 1024),
    )(numbers, tiles)


def solution(mesh):
    sizes = (mesh.shape["doc"], mesh.shape["term"], mesh.shape["pair"])
    in_specs = (
        P("doc", "term", None, None),
        P("doc", "term"),
        P("doc", "term"),
        P("doc"),
        P(("doc", "pair"), None),
        P(("doc", "pair")),
    )
    out_specs = P(("doc", "pair"), "term", None)
    return jax.shard_map(
        functools.partial(shards, sizes),
        mesh=mesh,
        in_specs=in_specs,
        out_specs=out_specs,
        check_vma=False,
    )
```

```python
import functools

import jax
import jax.numpy as jnp
from jax import lax
from jax.experimental import pallas as pl
from jax.experimental.pallas import tpu as pltpu
from jax.sharding import PartitionSpec as P

steps = 32767.0
tiny = 1e-30
saturation = 1.2
length_weight = 0.75
epsilon = 1e-06

MESH = pl.DeviceIdType.MESH


def exclusive_or(a, b, count):
    result, bit = 0, 1
    while bit < count:
        x, y = lax.rem(a // bit, 2), lax.rem(b // bit, 2)
        result = result + bit * (x + y - 2 * x * y)
        bit *= 2
    return result


def target_of(me, k, count):
    if count & (count - 1):
        return lax.rem(me + k, count)
    return exclusive_or(me, k, count)


def slot_of(me, owner, count):
    if count & (count - 1):
        return lax.rem(me - owner + count, count)
    return exclusive_or(me, owner, count)


def tiles_kernel(
    sizes,
    live_hbm,
    ids_hbm,
    counts_hbm,
    lengths_hbm,
    pairs_hbm,
    limit_ref,
    out_ref,
    tile_ref,
    live_ref,
    ids_ref,
    counts_ref,
    lengths_ref,
    pairs_ref,
    number_ref,
    masked,
    small,
    right_counts,
    left_weight,
    right_weight,
    aligned,
    ids_table,
    freq_table,
    length_table,
    partial_sum,
    coded,
    term_recv,
    side_own,
    side_recv,
    square_own,
    inverse_ref,
    final,
    pair_recv,
    load_sem,
    small_send_sem,
    small_recv_sem,
    count_send_sem,
    count_recv_sem,
    term_send_sem,
    term_recv_sem,
    side_send_sem,
    side_recv_sem,
    pair_send_sem,
    pair_recv_sem,
):
    n_doc, n_term, n_pair = sizes
    blocks, slots, rows, cols = counts_ref.shape
    per_core = blocks // n_pair
    n_right = n_doc * per_core
    part_rows = rows // n_term
    docs_all = n_doc * blocks * rows
    me_doc = lax.axis_index("doc")
    me_term = lax.axis_index("term")
    me_pair = lax.axis_index("pair")

    def doc_peer(k):
        return {"doc": target_of(me_doc, k, n_doc)}

    def term_peer(k):
        return {"term": target_of(me_term, k, n_term)}

    def pair_peer(k):
        return {"pair": lax.rem(me_pair + k, n_pair)}

    def small_copy(k):
        return pltpu.make_async_remote_copy(
            src_ref=small.at[0],
            dst_ref=small.at[k],
            send_sem=small_send_sem.at[k],
            recv_sem=small_recv_sem.at[k],
            device_id=doc_peer(k),
            device_id_type=MESH,
        )

    def count_copy(k):
        return pltpu.make_async_remote_copy(
            src_ref=masked.at[pl.ds(me_pair * per_core, per_core)],
            dst_ref=right_counts.at[k],
            send_sem=count_send_sem.at[k],
            recv_sem=count_recv_sem.at[k],
            device_id=doc_peer(k),
            device_id_type=MESH,
        )

    def term_copy(m, k):
        return pltpu.make_async_remote_copy(
            src_ref=coded.at[m, target_of(me_term, k, n_term)],
            dst_ref=term_recv.at[m, k],
            send_sem=term_send_sem.at[m, k],
            recv_sem=term_recv_sem.at[m, k],
            device_id=term_peer(k),
            device_id_type=MESH,
        )

    def side_copy(k):
        return pltpu.make_async_remote_copy(
            src_ref=side_own.at[target_of(me_term, k, n_term)],
            dst_ref=side_recv.at[k],
            send_sem=side_send_sem.at[k],
            recv_sem=side_recv_sem.at[k],
            device_id=term_peer(k),
            device_id_type=MESH,
        )

    def pair_copy(m, k):
        return pltpu.make_async_remote_copy(
            src_ref=final.at[m],
            dst_ref=pair_recv.at[k, m],
            send_sem=pair_send_sem.at[m, k],
            recv_sem=pair_recv_sem.at[m, k],
            device_id=pair_peer(k),
            device_id_type=MESH,
        )

    barrier = pltpu.get_barrier_semaphore()
    for k in range(1, n_doc):
        pl.semaphore_signal(barrier, inc=1, device_id=doc_peer(k), device_id_type=MESH)
    for k in range(1, n_term):
        pl.semaphore_signal(barrier, inc=1, device_id=term_peer(k), device_id_type=MESH)
    for k in range(1, n_pair):
        pl.semaphore_signal(barrier, inc=1, device_id=pair_peer(k), device_id_type=MESH)

    loads = [
        pltpu.make_async_copy(live_hbm, live_ref, load_sem.at[0]),
        pltpu.make_async_copy(ids_hbm, ids_ref, load_sem.at[1]),
        pltpu.make_async_copy(lengths_hbm, lengths_ref, load_sem.at[2]),
    ]
    extra = [pltpu.make_async_copy(pairs_hbm, pairs_ref, load_sem.at[3 + blocks])]
    loads += [
        pltpu.make_async_copy(counts_hbm.at[b], counts_ref.at[b], load_sem.at[3 + b])
        for b in range(blocks)
    ]
    for load in loads + extra:
        load.start()
    small[0] = jnp.zeros(small.shape[1:], jnp.float32)
    square_own[...] = jnp.zeros(square_own.shape, jnp.float32)
    out_ref[out_ref.shape[0] - 1] = jnp.zeros(out_ref.shape[1:], jnp.float32)
    for load in loads[:3]:
        load.wait()
    for b in range(blocks):
        loads[3 + b].wait()
        for s in range(slots):
            live = jnp.broadcast_to(live_ref[b : b + 1, s : s + 1], (rows, cols)) > 0
            value = jnp.where(live, counts_ref[b, s].astype(jnp.float32), 0.0)
            masked[b, s] = value.astype(jnp.bfloat16)
            small[0, b, s : s + 1] = jnp.sum(
                jnp.where(value > 0.0, 1.0, 0.0), axis=0, keepdims=True
            )
            small[0, b, slots + s : slots + s + 1] = jnp.broadcast_to(
                ids_ref[b : b + 1, s : s + 1], (1, cols)
            ).astype(jnp.float32)
    small[0, blocks, 0:blocks] = lengths_ref[...].astype(jnp.float32)

    pl.semaphore_wait(barrier, n_doc + n_term + n_pair - 3)

    for k in range(1, n_doc):
        small_copy(k).start()
    for k in sorted(range(1, n_doc), key=lambda k: k & (k - 1) != 0):
        count_copy(k).start()
    for k in range(1, n_doc):
        small_copy(k).wait_recv()

    row_at = lax.broadcasted_iota(jnp.int32, (rows, cols), 0)
    col_at = lax.broadcasted_iota(jnp.int32, (rows, cols), 1)
    diagonal = row_at == col_at
    part_diagonal = row_at[:part_rows] + me_term * part_rows == col_at[:part_rows]
    total_len = lax.fori_loop(
        0,
        n_doc,
        lambda k, acc: acc + jnp.sum(small[k, blocks], axis=0, keepdims=True),
        jnp.zeros((1, cols), jnp.float32),
    )
    avg_len = jnp.sum(total_len, axis=1, keepdims=True) / docs_all

    def table_row(k, b, place):
        ids_table[pl.ds(place * slots, slots)] = small[k, b, slots : 2 * slots]
        length = small[k, blocks, pl.ds(b, 1)]
        scale = saturation * (1.0 - length_weight + length_weight * length / avg_len)
        scale = jnp.sum(jnp.where(diagonal, scale, 0.0), axis=1, keepdims=True)
        length_table[place] = jnp.broadcast_to(scale, (rows, cols))

    for b in range(blocks):
        table_row(0, b, b)

    def right_rows(k, carry):
        for i in range(per_core):
            table_row(k, me_pair * per_core + i, blocks + k * per_core + i)
        return carry

    lax.fori_loop(0, n_doc, right_rows, 0, unroll=min(n_doc, 4))
    ids = ids_table[...]

    def add(k, acc):
        for b in range(blocks):
            table = small[k, b]
            for s in range(slots):
                same = ids == table[slots + s : slots + s + 1]
                acc = acc + jnp.where(same, table[s : s + 1], 0.0)
        return acc

    doc_freq = lax.fori_loop(
        0, n_doc, add, jnp.zeros(ids.shape, jnp.float32), unroll=min(n_doc, 4)
    )
    freq_table[...] = jnp.log(1.0 + (docs_all - doc_freq + 0.5) / (doc_freq + 0.5)) * (
        saturation + 1.0
    )

    def weigh(read, target, place):
        squares = jnp.zeros((rows, cols), jnp.float32)
        for s in range(slots):
            freq = read(s).astype(jnp.float32)
            weight = freq_table[pl.ds(place * slots + s, 1)] * freq / (freq + length_table[place])
            squares = squares + weight * weight
            target[s] = weight.astype(jnp.bfloat16)
        return squares

    def keep_squares(squares, place):
        squares = jnp.sum(squares, axis=1, keepdims=True)
        squares = jnp.where(diagonal, squares, 0.0)
        square_own[pl.ds(place, 1)] = jnp.sum(squares, axis=0, keepdims=True)

    def align(m, right_ids):
        for b in range(blocks):
            left_ids = small[0, b, slots : 2 * slots]
            for j in range(slots):
                total = jnp.zeros((rows, cols), jnp.bfloat16)
                for i in range(slots):
                    same = left_ids[i : i + 1] == right_ids[j : j + 1]
                    same = jnp.where(same, 1.0, 0.0).astype(jnp.bfloat16)
                    total = total + left_weight[b, i] * same
                aligned[m, b * rows : (b + 1) * rows, j * cols : (j + 1) * cols] = total

    def grams(m, right):
        gram = lax.dot_general(
            aligned[m],
            jnp.concatenate([right[j] for j in range(slots)], axis=1),
            (((1,), (1,)), ((), ())),
            preferred_element_type=jnp.float32,
        )
        for z in range(n_term):
            for b in range(blocks):
                start = b * rows + z * part_rows
                piece = gram[start : start + part_rows]
                top = jnp.maximum(jnp.max(piece, axis=0, keepdims=True), tiny)
                partial_sum[m, z, b] = piece
                code = (piece * (steps / top) + 0.5).astype(jnp.int32)
                coded[m, z, b] = code.astype(jnp.int16)
                side_own[z, pl.ds(m * blocks + b, 1)] = top * (1.0 / steps)
        for k in reversed(range(1, n_term)):
            term_copy(m, k).start()

    left_squares = [
        weigh(lambda s, b=b: masked[b, s], left_weight.at[b], b) for b in range(blocks)
    ]
    for i in range(per_core):
        own = me_pair * per_core + i
        align(i, small[0, own, slots : 2 * slots])
        grams(i, left_weight.at[own])

    def align_right(k, carry):
        for i in range(per_core):
            align(k * per_core + i, small[k, me_pair * per_core + i, slots : 2 * slots])
        return carry

    lax.fori_loop(1, n_doc, align_right, 0)
    for load in extra:
        load.wait()
    left = pairs_ref[0:1]
    right = pairs_ref[1:2]
    number = left - me_doc * blocks
    for block in range(n_doc * blocks):
        owner, inner = block // blocks, block % blocks
        side = lax.rem(me_pair - inner // per_core + n_pair, n_pair)
        m = slot_of(me_doc, owner, n_doc) * per_core + inner % per_core
        number = number + jnp.where(right == block, (side * n_right + m) * blocks, 0)
    row = lax.broadcasted_iota(jnp.int32, number.shape, 1)
    number_ref[...] = jnp.where(row < limit_ref[0], number, out_ref.shape[0] - 1)
    number_copy = pltpu.make_async_copy(number_ref, tile_ref, load_sem.at[4 + blocks])
    number_copy.start()

    for b in range(blocks):
        keep_squares(left_squares[b], b)
    for i in range(per_core):
        square_own[pl.ds(blocks + i, 1)] = square_own[pl.ds(me_pair * per_core + i, 1)]

    def right_step(k, carry):
        count_copy(k).wait_recv()
        for i in range(per_core):
            m = k * per_core + i
            squares = weigh(lambda s, i=i: right_counts[k, i, s], right_weight, blocks + m)
            grams(m, right_weight)
            keep_squares(squares, blocks + m)
        return carry

    lax.fori_loop(1, n_doc, right_step, 0)

    scale_rows = side_own.shape[1] - square_own.shape[0]
    squares = square_own[...]
    for z in range(n_term):
        side_own[z, scale_rows:] = squares
    for k in reversed(range(1, n_term)):
        side_copy(k).start()
    for k in range(1, n_term):
        side_copy(k).wait_recv()
        squares = squares + side_recv[k, scale_rows:]
    inverse = lax.rsqrt(squares + epsilon)
    inverse_ref[...] = inverse
    left_scale = []
    for b in range(blocks):
        picked = jnp.where(part_diagonal, inverse[b : b + 1], 0.0)
        left_scale.append(jnp.sum(picked, axis=1, keepdims=True))

    def finish(m, carry):
        for k in range(1, n_term):
            term_copy(m, k).wait_recv()
        right_scale = inverse_ref[pl.ds(blocks + m, 1)]
        for b in range(blocks):
            total = partial_sum[m, me_term, b]
            for k in range(1, n_term):
                scale = side_recv[k, pl.ds(m * blocks + b, 1)]
                total = total + term_recv[m, k, b].astype(jnp.float32) * scale
            value = total * left_scale[b] * right_scale
            final[m, b] = value
            out_ref[m * blocks + b] = value
        for k in range(1, n_pair):
            pair_copy(m, k).start()
        return carry

    lax.fori_loop(0, n_right, finish, 0)

    def collect(m, carry):
        for k in range(1, n_pair):
            pair_copy(m, k).wait_recv()
            out_ref[pl.ds((k * n_right + m) * blocks, blocks)] = pair_recv[k, m]
        for k in range(1, n_term):
            term_copy(m, k).wait_send()
        for k in range(1, n_pair):
            pair_copy(m, k).wait_send()
        return carry

    lax.fori_loop(0, n_right, collect, 0)
    number_copy.wait()
    for k in range(1, n_term):
        side_copy(k).wait_send()
    for k in range(1, n_doc):
        small_copy(k).wait_send()
        count_copy(k).wait_send()


def place_kernel(tile_ref, tiles_ref, out_ref, sem):
    def step(row, carry):
        tile = tile_ref[0, row]
        pltpu.make_async_copy(tiles_ref.at[tile], out_ref.at[row], sem).start()
        return carry

    lax.fori_loop(0, out_ref.shape[0], step, 0, unroll=8)
    pltpu.make_async_copy(out_ref, out_ref, sem).wait()


def shards(sizes, counts, block_ids, live_slots, lengths, pairs, pair_count):
    n_doc, n_term, n_pair = sizes
    blocks, slots, rows, cols = counts.shape
    per_core = blocks // n_pair
    n_right = n_doc * per_core
    part_rows = rows // n_term
    table_rows = -(-max(2 * slots, blocks) // 8) * 8
    square_rows = -(-(blocks + n_right) // 8) * 8
    dma = pltpu.SemaphoreType.DMA
    scale_rows = -(-(blocks * n_right) // 8) * 8
    hbm = pl.BlockSpec(memory_space=pltpu.HBM)
    smem = pl.BlockSpec(memory_space=pltpu.SMEM)
    vmem = pl.BlockSpec(memory_space=pltpu.VMEM)
    tiles, numbers = pl.pallas_call(
        functools.partial(tiles_kernel, sizes),
        out_shape=(
            pltpu.VMEM((n_pair * n_right * blocks + 1, part_rows, rows), jnp.float32),
            pltpu.SMEM((1, pairs.shape[0]), jnp.int32),
        ),
        in_specs=[hbm] * 5 + [smem],
        out_specs=(vmem, smem),
        scratch_shapes=[
            pltpu.VMEM((blocks, slots), jnp.int32),
            pltpu.VMEM((blocks, slots), jnp.int32),
            pltpu.VMEM((blocks, slots, rows, cols), jnp.int32),
            pltpu.VMEM((blocks, rows), jnp.int32),
            pltpu.VMEM((2, pairs.shape[0]), jnp.int32),
            pltpu.VMEM((1, pairs.shape[0]), jnp.int32),
            pltpu.VMEM((blocks, slots, rows, cols), jnp.bfloat16),
            pltpu.VMEM((n_doc, blocks + 1, table_rows, cols), jnp.float32),
            pltpu.VMEM((n_doc, per_core, slots, rows, cols), jnp.bfloat16),
            pltpu.VMEM((blocks, slots, rows, cols), jnp.bfloat16),
            pltpu.VMEM((slots, rows, cols), jnp.bfloat16),
            pltpu.VMEM((n_right, blocks * rows, slots * cols), jnp.bfloat16),
            pltpu.VMEM(((blocks + n_right) * slots, cols), jnp.float32),
            pltpu.VMEM(((blocks + n_right) * slots, cols), jnp.float32),
            pltpu.VMEM((blocks + n_right, rows, rows), jnp.float32),
            pltpu.VMEM((n_right, n_term, blocks, part_rows, rows), jnp.float32),
            pltpu.VMEM((n_right, n_term, blocks, part_rows, rows), jnp.int16),
            pltpu.VMEM((n_right, n_term, blocks, part_rows, rows), jnp.int16),
            pltpu.VMEM((n_term, scale_rows + square_rows, rows), jnp.float32),
            pltpu.VMEM((n_term, scale_rows + square_rows, rows), jnp.float32),
            pltpu.VMEM((square_rows, rows), jnp.float32),
            pltpu.VMEM((square_rows, rows), jnp.float32),
            pltpu.VMEM((n_right, blocks, part_rows, rows), jnp.float32),
            pltpu.VMEM((n_pair, n_right, blocks, part_rows, rows), jnp.float32),
            dma((5 + blocks,)),
            dma((n_doc,)),
            dma((n_doc,)),
            dma((n_doc,)),
            dma((n_doc,)),
            dma((n_right, n_term)),
            dma((n_right, n_term)),
            dma((n_term,)),
            dma((n_term,)),
            dma((n_right, n_pair)),
            dma((n_right, n_pair)),
        ],
        compiler_params=pltpu.CompilerParams(
            collective_id=0, has_side_effects=True, vmem_limit_bytes=48 * 1024 * 1024
        ),
    )(*[pltpu.with_memory_space_constraint(x, pltpu.HBM) for x in (live_slots, block_ids, counts, lengths.reshape(blocks, rows), pairs.T)], pair_count)
    return pl.pallas_call(
        place_kernel,
        out_shape=jax.ShapeDtypeStruct((pairs.shape[0], part_rows, rows), jnp.float32),
        in_specs=[smem, pl.BlockSpec(memory_space=pl.ANY)],
        out_specs=hbm,
        scratch_shapes=[dma(())],
        compiler_params=pltpu.CompilerParams(vmem_limit_bytes=48 * 1024 * 1024),
    )(numbers, tiles)


def solution(mesh):
    sizes = (mesh.shape["doc"], mesh.shape["term"], mesh.shape["pair"])
    in_specs = (
        P("doc", "term", None, None),
        P("doc", "term"),
        P("doc", "term"),
        P("doc"),
        P(("doc", "pair"), None),
        P(("doc", "pair")),
    )
    out_specs = P(("doc", "pair"), "term", None)
    return jax.shard_map(
        functools.partial(shards, sizes),
        mesh=mesh,
        in_specs=in_specs,
        out_specs=out_specs,
        check_vma=False,
    )
```

```python
import functools

import jax
import jax.numpy as jnp
from jax import lax
from jax.experimental import pallas as pl
from jax.experimental.pallas import tpu as pltpu
from jax.sharding import PartitionSpec as P

steps = 32767.0
tiny = 1e-30
saturation = 1.2
length_weight = 0.75
epsilon = 1e-06

MESH = pl.DeviceIdType.MESH


def exclusive_or(a, b, count):
    result, bit = 0, 1
    while bit < count:
        x, y = lax.rem(a // bit, 2), lax.rem(b // bit, 2)
        result = result + bit * (x + y - 2 * x * y)
        bit *= 2
    return result


def target_of(me, k, count):
    if count & (count - 1):
        return lax.rem(me + k, count)
    return exclusive_or(me, k, count)


def slot_of(me, owner, count):
    if count & (count - 1):
        return lax.rem(me - owner + count, count)
    return exclusive_or(me, owner, count)


def tiles_kernel(
    sizes,
    live_hbm,
    ids_hbm,
    counts_hbm,
    lengths_hbm,
    pairs_hbm,
    limit_ref,
    out_ref,
    tile_ref,
    live_ref,
    ids_ref,
    counts_ref,
    lengths_ref,
    pairs_ref,
    number_ref,
    masked,
    small,
    right_counts,
    left_weight,
    right_weight,
    aligned,
    ids_table,
    freq_table,
    length_table,
    partial_sum,
    coded,
    term_recv,
    side_own,
    side_recv,
    square_own,
    inverse_ref,
    final,
    pair_recv,
    load_sem,
    small_send_sem,
    small_recv_sem,
    count_send_sem,
    count_recv_sem,
    term_send_sem,
    term_recv_sem,
    side_send_sem,
    side_recv_sem,
    pair_send_sem,
    pair_recv_sem,
):
    n_doc, n_term, n_pair = sizes
    blocks, slots, rows, cols = counts_ref.shape
    per_core = blocks // n_pair
    n_right = n_doc * per_core
    part_rows = rows // n_term
    docs_all = n_doc * blocks * rows
    me_doc = lax.axis_index("doc")
    me_term = lax.axis_index("term")
    me_pair = lax.axis_index("pair")

    def doc_peer(k):
        return {"doc": target_of(me_doc, k, n_doc)}

    def term_peer(k):
        return {"term": lax.rem(me_term + k, n_term)}

    def pair_peer(k):
        return {"pair": lax.rem(me_pair + k, n_pair)}

    def small_copy(k):
        return pltpu.make_async_remote_copy(
            src_ref=small.at[0],
            dst_ref=small.at[k],
            send_sem=small_send_sem.at[k],
            recv_sem=small_recv_sem.at[k],
            device_id=doc_peer(k),
            device_id_type=MESH,
        )

    def count_copy(k):
        return pltpu.make_async_remote_copy(
            src_ref=masked.at[pl.ds(me_pair * per_core, per_core)],
            dst_ref=right_counts.at[k],
            send_sem=count_send_sem.at[k],
            recv_sem=count_recv_sem.at[k],
            device_id=doc_peer(k),
            device_id_type=MESH,
        )

    relay = False
    near = 1 + lax.rem(me_pair, 2)
    far = 3 - near

    def relay_copy():
        return pltpu.make_async_remote_copy(
            src_ref=right_counts.at[near],
            dst_ref=right_counts.at[3],
            send_sem=count_send_sem.at[3],
            recv_sem=count_recv_sem.at[3],
            device_id=doc_peer(far),
            device_id_type=MESH,
        )

    def term_copy(m, k):
        return pltpu.make_async_remote_copy(
            src_ref=coded.at[m, lax.rem(me_term + k, n_term)],
            dst_ref=term_recv.at[m, k],
            send_sem=term_send_sem.at[m, k],
            recv_sem=term_recv_sem.at[m, k],
            device_id=term_peer(k),
            device_id_type=MESH,
        )

    def side_copy(k):
        return pltpu.make_async_remote_copy(
            src_ref=side_own.at[lax.rem(me_term + k, n_term)],
            dst_ref=side_recv.at[k],
            send_sem=side_send_sem.at[k],
            recv_sem=side_recv_sem.at[k],
            device_id=term_peer(k),
            device_id_type=MESH,
        )

    def pair_copy(m, k):
        return pltpu.make_async_remote_copy(
            src_ref=final.at[m],
            dst_ref=pair_recv.at[k, m],
            send_sem=pair_send_sem.at[m, k],
            recv_sem=pair_recv_sem.at[m, k],
            device_id=pair_peer(k),
            device_id_type=MESH,
        )

    barrier = pltpu.get_barrier_semaphore()
    for k in range(1, n_doc):
        pl.semaphore_signal(barrier, inc=1, device_id=doc_peer(k), device_id_type=MESH)
    for k in range(1, n_term):
        pl.semaphore_signal(barrier, inc=1, device_id=term_peer(k), device_id_type=MESH)
    for k in range(1, n_pair):
        pl.semaphore_signal(barrier, inc=1, device_id=pair_peer(k), device_id_type=MESH)

    loads = [
        pltpu.make_async_copy(live_hbm, live_ref, load_sem.at[0]),
        pltpu.make_async_copy(ids_hbm, ids_ref, load_sem.at[1]),
        pltpu.make_async_copy(lengths_hbm, lengths_ref, load_sem.at[2]),
    ]
    extra = [pltpu.make_async_copy(pairs_hbm, pairs_ref, load_sem.at[3 + blocks])]
    loads += [
        pltpu.make_async_copy(counts_hbm.at[b], counts_ref.at[b], load_sem.at[3 + b])
        for b in range(blocks)
    ]
    for load in loads + extra:
        load.start()
    small[0] = jnp.zeros(small.shape[1:], jnp.float32)
    square_own[...] = jnp.zeros(square_own.shape, jnp.float32)
    out_ref[out_ref.shape[0] - 1] = jnp.zeros(out_ref.shape[1:], jnp.float32)
    for load in loads[:3]:
        load.wait()
    for b in range(blocks):
        loads[3 + b].wait()
        for s in range(slots):
            live = jnp.broadcast_to(live_ref[b : b + 1, s : s + 1], (rows, cols)) > 0
            value = jnp.where(live, counts_ref[b, s].astype(jnp.float32), 0.0)
            masked[b, s] = value.astype(jnp.bfloat16)
            small[0, b, s : s + 1] = jnp.sum(
                jnp.where(value > 0.0, 1.0, 0.0), axis=0, keepdims=True
            )
            small[0, b, slots + s : slots + s + 1] = jnp.broadcast_to(
                ids_ref[b : b + 1, s : s + 1], (1, cols)
            ).astype(jnp.float32)
    small[0, blocks, 0:blocks] = lengths_ref[...].astype(jnp.float32)

    pl.semaphore_wait(barrier, n_doc + n_term + n_pair - 3)

    for k in range(1, n_doc):
        small_copy(k).start()
    for k in (near, far) if relay else range(1, n_doc):
        count_copy(k).start()
    for k in range(1, n_doc):
        small_copy(k).wait_recv()

    row_at = lax.broadcasted_iota(jnp.int32, (rows, cols), 0)
    col_at = lax.broadcasted_iota(jnp.int32, (rows, cols), 1)
    diagonal = row_at == col_at
    part_diagonal = row_at[:part_rows] + me_term * part_rows == col_at[:part_rows]
    total_len = lax.fori_loop(
        0,
        n_doc,
        lambda k, acc: acc + jnp.sum(small[k, blocks], axis=0, keepdims=True),
        jnp.zeros((1, cols), jnp.float32),
    )
    avg_len = jnp.sum(total_len, axis=1, keepdims=True) / docs_all

    def table_row(k, b, place):
        ids_table[pl.ds(place * slots, slots)] = small[k, b, slots : 2 * slots]
        length = small[k, blocks, pl.ds(b, 1)]
        scale = saturation * (1.0 - length_weight + length_weight * length / avg_len)
        scale = jnp.sum(jnp.where(diagonal, scale, 0.0), axis=1, keepdims=True)
        length_table[place] = jnp.broadcast_to(scale, (rows, cols))

    for b in range(blocks):
        table_row(0, b, b)

    def right_rows(k, carry):
        for i in range(per_core):
            table_row(k, me_pair * per_core + i, blocks + k * per_core + i)
        return carry

    lax.fori_loop(0, n_doc, right_rows, 0, unroll=min(n_doc, 4))
    ids = ids_table[...]

    def add(k, acc):
        for b in range(blocks):
            table = small[k, b]
            for s in range(slots):
                same = ids == table[slots + s : slots + s + 1]
                acc = acc + jnp.where(same, table[s : s + 1], 0.0)
        return acc

    doc_freq = lax.fori_loop(
        0, n_doc, add, jnp.zeros(ids.shape, jnp.float32), unroll=min(n_doc, 4)
    )
    freq_table[...] = jnp.log(1.0 + (docs_all - doc_freq + 0.5) / (doc_freq + 0.5)) * (
        saturation + 1.0
    )

    def weigh(read, target, place):
        squares = jnp.zeros((rows, cols), jnp.float32)
        for s in range(slots):
            freq = read(s).astype(jnp.float32)
            weight = freq_table[pl.ds(place * slots + s, 1)] * freq / (freq + length_table[place])
            squares = squares + weight * weight
            target[s] = weight.astype(jnp.bfloat16)
        return squares

    def keep_squares(squares, place):
        squares = jnp.sum(squares, axis=1, keepdims=True)
        squares = jnp.where(diagonal, squares, 0.0)
        square_own[pl.ds(place, 1)] = jnp.sum(squares, axis=0, keepdims=True)

    def align(m, right_ids):
        for b in range(blocks):
            left_ids = small[0, b, slots : 2 * slots]
            for j in range(slots):
                total = jnp.zeros((rows, cols), jnp.bfloat16)
                for i in range(slots):
                    same = left_ids[i : i + 1] == right_ids[j : j + 1]
                    same = jnp.where(same, 1.0, 0.0).astype(jnp.bfloat16)
                    total = total + left_weight[b, i] * same
                aligned[m, b * rows : (b + 1) * rows, j * cols : (j + 1) * cols] = total

    def grams(m, right):
        gram = lax.dot_general(
            aligned[m],
            jnp.concatenate([right[j] for j in range(slots)], axis=1),
            (((1,), (1,)), ((), ())),
            preferred_element_type=jnp.float32,
        )
        for z in range(n_term):
            for b in range(blocks):
                start = b * rows + z * part_rows
                piece = gram[start : start + part_rows]
                top = jnp.maximum(jnp.max(piece, axis=0, keepdims=True), tiny)
                partial_sum[m, z, b] = piece
                code = (piece * (steps / top) + 0.5).astype(jnp.int32)
                coded[m, z, b] = code.astype(jnp.int16)
                side_own[z, pl.ds(m * blocks + b, 1)] = top * (1.0 / steps)
        for k in range(1, n_term):
            term_copy(m, k).start()

    left_squares = [
        weigh(lambda s, b=b: masked[b, s], left_weight.at[b], b) for b in range(blocks)
    ]
    for i in range(per_core):
        own = me_pair * per_core + i
        align(i, small[0, own, slots : 2 * slots])
        grams(i, left_weight.at[own])
    if relay:
        count_copy(near).wait_recv()
        relay_copy().start()

    def align_right(k, carry):
        for i in range(per_core):
            align(k * per_core + i, small[k, me_pair * per_core + i, slots : 2 * slots])
        return carry

    lax.fori_loop(1, n_doc, align_right, 0)
    for load in extra:
        load.wait()
    left = pairs_ref[0:1]
    right = pairs_ref[1:2]
    number = left - me_doc * blocks
    for block in range(n_doc * blocks):
        owner, inner = block // blocks, block % blocks
        side = lax.rem(me_pair - inner // per_core + n_pair, n_pair)
        m = slot_of(me_doc, owner, n_doc) * per_core + inner % per_core
        number = number + jnp.where(right == block, (side * n_right + m) * blocks, 0)
    row = lax.broadcasted_iota(jnp.int32, number.shape, 1)
    number_ref[...] = jnp.where(row < limit_ref[0], number, out_ref.shape[0] - 1)
    number_copy = pltpu.make_async_copy(number_ref, tile_ref, load_sem.at[4 + blocks])
    number_copy.start()

    for b in range(blocks):
        keep_squares(left_squares[b], b)
    for i in range(per_core):
        square_own[pl.ds(blocks + i, 1)] = square_own[pl.ds(me_pair * per_core + i, 1)]

    def right_step(step, carry):
        if relay:
            k = jnp.where(step == 1, near, jnp.where(step == 2, far, 3))

            @pl.when(step == 2)
            def _():
                count_copy(far).wait_recv()

            @pl.when(step == 3)
            def _():
                relay_copy().wait_recv()
        else:
            k = step
            count_copy(k).wait_recv()
        for i in range(per_core):
            m = k * per_core + i
            squares = weigh(lambda s, i=i: right_counts[k, i, s], right_weight, blocks + m)
            grams(m, right_weight)
            keep_squares(squares, blocks + m)
        return carry

    lax.fori_loop(1, n_doc, right_step, 0)

    scale_rows = side_own.shape[1] - square_own.shape[0]
    squares = square_own[...]
    for z in range(n_term):
        side_own[z, scale_rows:] = squares
    for k in range(1, n_term):
        side_copy(k).start()
    for k in range(1, n_term):
        side_copy(k).wait_recv()
        squares = squares + side_recv[k, scale_rows:]
    inverse = lax.rsqrt(squares + epsilon)
    inverse_ref[...] = inverse
    left_scale = []
    for b in range(blocks):
        picked = jnp.where(part_diagonal, inverse[b : b + 1], 0.0)
        left_scale.append(jnp.sum(picked, axis=1, keepdims=True))

    def finish(m, carry):
        for k in range(1, n_term):
            term_copy(m, k).wait_recv()
        right_scale = inverse_ref[pl.ds(blocks + m, 1)]
        for b in range(blocks):
            total = partial_sum[m, me_term, b]
            for k in range(1, n_term):
                scale = side_recv[k, pl.ds(m * blocks + b, 1)]
                total = total + term_recv[m, k, b].astype(jnp.float32) * scale
            value = total * left_scale[b] * right_scale
            final[m, b] = value
            out_ref[m * blocks + b] = value
        for k in range(1, n_pair):
            pair_copy(m, k).start()
        return carry

    lax.fori_loop(0, n_right, finish, 0, unroll=min(n_right, 4))

    def collect(m, carry):
        for k in range(1, n_pair):
            pair_copy(m, k).wait_recv()
            out_ref[pl.ds((k * n_right + m) * blocks, blocks)] = pair_recv[k, m]
        for k in range(1, n_term):
            term_copy(m, k).wait_send()
        for k in range(1, n_pair):
            pair_copy(m, k).wait_send()
        return carry

    lax.fori_loop(0, n_right, collect, 0, unroll=min(n_right, 4))
    number_copy.wait()
    for k in range(1, n_term):
        side_copy(k).wait_send()
    for k in range(1, n_doc):
        small_copy(k).wait_send()
        if relay and k == 3:
            relay_copy().wait_send()
        else:
            count_copy(k).wait_send()


def place_kernel(tile_ref, tiles_ref, out_ref, sem):
    def step(row, carry):
        tile = tile_ref[0, row]
        pltpu.make_async_copy(tiles_ref.at[tile], out_ref.at[row], sem).start()
        return carry

    lax.fori_loop(0, out_ref.shape[0], step, 0, unroll=8)
    pltpu.make_async_copy(out_ref, out_ref, sem).wait()


def shards(sizes, counts, block_ids, live_slots, lengths, pairs, pair_count):
    n_doc, n_term, n_pair = sizes
    blocks, slots, rows, cols = counts.shape
    per_core = blocks // n_pair
    n_right = n_doc * per_core
    part_rows = rows // n_term
    table_rows = -(-max(2 * slots, blocks) // 8) * 8
    square_rows = -(-(blocks + n_right) // 8) * 8
    dma = pltpu.SemaphoreType.DMA
    scale_rows = -(-(blocks * n_right) // 8) * 8
    hbm = pl.BlockSpec(memory_space=pltpu.HBM)
    smem = pl.BlockSpec(memory_space=pltpu.SMEM)
    vmem = pl.BlockSpec(memory_space=pltpu.VMEM)
    tiles, numbers = pl.pallas_call(
        functools.partial(tiles_kernel, sizes),
        out_shape=(
            pltpu.VMEM((n_pair * n_right * blocks + 1, part_rows, rows), jnp.float32),
            pltpu.SMEM((1, pairs.shape[0]), jnp.int32),
        ),
        in_specs=[hbm] * 5 + [smem],
        out_specs=(vmem, smem),
        scratch_shapes=[
            pltpu.VMEM((blocks, slots), jnp.int32),
            pltpu.VMEM((blocks, slots), jnp.int32),
            pltpu.VMEM((blocks, slots, rows, cols), jnp.int32),
            pltpu.VMEM((blocks, rows), jnp.int32),
            pltpu.VMEM((2, pairs.shape[0]), jnp.int32),
            pltpu.VMEM((1, pairs.shape[0]), jnp.int32),
            pltpu.VMEM((blocks, slots, rows, cols), jnp.bfloat16),
            pltpu.VMEM((n_doc, blocks + 1, table_rows, cols), jnp.float32),
            pltpu.VMEM((n_doc, per_core, slots, rows, cols), jnp.bfloat16),
            pltpu.VMEM((blocks, slots, rows, cols), jnp.bfloat16),
            pltpu.VMEM((slots, rows, cols), jnp.bfloat16),
            pltpu.VMEM((n_right, blocks * rows, slots * cols), jnp.bfloat16),
            pltpu.VMEM(((blocks + n_right) * slots, cols), jnp.float32),
            pltpu.VMEM(((blocks + n_right) * slots, cols), jnp.float32),
            pltpu.VMEM((blocks + n_right, rows, rows), jnp.float32),
            pltpu.VMEM((n_right, n_term, blocks, part_rows, rows), jnp.float32),
            pltpu.VMEM((n_right, n_term, blocks, part_rows, rows), jnp.int16),
            pltpu.VMEM((n_right, n_term, blocks, part_rows, rows), jnp.int16),
            pltpu.VMEM((n_term, scale_rows + square_rows, rows), jnp.float32),
            pltpu.VMEM((n_term, scale_rows + square_rows, rows), jnp.float32),
            pltpu.VMEM((square_rows, rows), jnp.float32),
            pltpu.VMEM((square_rows, rows), jnp.float32),
            pltpu.VMEM((n_right, blocks, part_rows, rows), jnp.float32),
            pltpu.VMEM((n_pair, n_right, blocks, part_rows, rows), jnp.float32),
            dma((5 + blocks,)),
            dma((n_doc,)),
            dma((n_doc,)),
            dma((n_doc,)),
            dma((n_doc,)),
            dma((n_right, n_term)),
            dma((n_right, n_term)),
            dma((n_term,)),
            dma((n_term,)),
            dma((n_right, n_pair)),
            dma((n_right, n_pair)),
        ],
        compiler_params=pltpu.CompilerParams(
            collective_id=0, has_side_effects=True, vmem_limit_bytes=48 * 1024 * 1024
        ),
    )(*[pltpu.with_memory_space_constraint(x, pltpu.HBM) for x in (live_slots, block_ids, counts, lengths.reshape(blocks, rows), pairs.T)], pair_count)
    return pl.pallas_call(
        place_kernel,
        out_shape=jax.ShapeDtypeStruct((pairs.shape[0], part_rows, rows), jnp.float32),
        in_specs=[smem, pl.BlockSpec(memory_space=pl.ANY)],
        out_specs=hbm,
        scratch_shapes=[dma(())],
        compiler_params=pltpu.CompilerParams(vmem_limit_bytes=48 * 1024 * 1024),
    )(numbers, tiles)


def solution(mesh):
    sizes = (mesh.shape["doc"], mesh.shape["term"], mesh.shape["pair"])
    in_specs = (
        P("doc", "term", None, None),
        P("doc", "term"),
        P("doc", "term"),
        P("doc"),
        P(("doc", "pair"), None),
        P(("doc", "pair")),
    )
    out_specs = P(("doc", "pair"), "term", None)
    return jax.shard_map(
        functools.partial(shards, sizes),
        mesh=mesh,
        in_specs=in_specs,
        out_specs=out_specs,
        check_vma=False,
    )
```
